256 devices in a mesh: outer: 4 (over z_hi, core), dp: 64 (over y, z_lo, x).
Axes of the slice: x: 4, y: 4, z: 8 (z_hi: 2, z_lo: 4; z = z_hi * 4 + z_lo), core: 2. Of those that a mesh axis runs over, the one named last changes fastest.
Arguments:
- gradients: bfloat16 [4, 64, 256, 128, 128], P('outer', 'dp'), may hold values from -6 to 6
- sign_flips: int32 [128, 128], replicated, may hold values from -1 to 1, as said below
Outputs:
- mean_code: float32 [256, 128, 128], P('dp', 'outer')
- gradient_sum: bfloat16 [256, 128, 128], replicated
The draws below stay inside these ranges and needn't reach their ends.
Inputs may be any that keep to these rules, and one draw needn't show every extreme that they name: `sign_flips`: each entry is -1 or +1.
All inputs are finite; a program needn't handle non-finite values.
Results may differ from the reference program's by a relative error of at most 0.0029.
Values may be sent and summed in bfloat16 or wider, within the bound.
No kernel may reach another device: no remote copies, remote signals or barrier semaphores. Data moves between devices by JAX's collectives and lax.ppermute only.
A program may use at most 128 MiB of HBM per device.

```python
import jax
import jax.numpy as jnp
from jax import lax

PASS = 128
BLOCKS = 256
WORKERS = 256
N_OUTER = 4
N_DP = 64


def draw_gradients(key, part):
    key = jax.random.fold_in(key, 11)
    noise_key = jax.random.fold_in(key, 1)
    worker = jnp.arange(WORKERS, dtype=jnp.float32)
    ramp = jnp.power(3.0, worker / float(WORKERS - 1))
    shape_all = (WORKERS, BLOCKS, PASS, PASS)
    noise = jnp.clip(jax.random.normal(noise_key, shape_all, jnp.float32), -6.0, 6.0)
    values = 0.0625 * ramp[:, None, None, None] * noise
    return values.reshape(N_OUTER, N_DP, BLOCKS, PASS, PASS).astype(jnp.bfloat16)


def draw_sign_flips(key, part):
    key = jax.random.fold_in(key, 23)
    bits_drawn = jax.random.randint(key, (PASS, PASS), 0, 2, dtype=jnp.int32)
    return (2 * bits_drawn - 1).astype(jnp.int32)


def setup_inputs(seed: int = 0) -> dict:
    streams_of = jax.random.split(jax.random.key(seed), 3)
    return {
        "gradients": draw_gradients(jax.random.fold_in(streams_of[2], 71), 0),
        "sign_flips": draw_sign_flips(jax.random.fold_in(streams_of[2], 71), 0),
    }


def hadamard(length):
    index_row = jnp.arange(length, dtype=jnp.int32)[:, None]
    index_col = jnp.arange(length, dtype=jnp.int32)[None, :]
    common_bits = index_row & index_col
    parity = jnp.zeros((length, length), jnp.int32)
    for bit_pos in range(length.bit_length() - 1):
        parity = parity + ((common_bits >> bit_pos) & 1)
    return (1 - 2 * (parity % 2)).astype(jnp.float32)


def rotate(blocks_f, sign_f, hadamard_mat):
    length = hadamard_mat.shape[0]
    flipped = blocks_f * sign_f
    first_pass = jnp.einsum("bij,jk->bik", flipped, hadamard_mat, precision=lax.Precision.HIGHEST)
    return jnp.einsum("ij,bjk->bik", hadamard_mat, first_pass, precision=lax.Precision.HIGHEST) / float(length)


def quantize(rotated, maximum):
    return jnp.floor(rotated * (127.0 / maximum) + 0.5).astype(jnp.bfloat16)


def decode(code_total, sign_f, hadamard_mat, maximum):
    length = hadamard_mat.shape[0]
    first_pass = jnp.einsum("bij,jk->bik", code_total, hadamard_mat, precision=lax.Precision.HIGHEST)
    second_pass = jnp.einsum("ij,bjk->bik", hadamard_mat, first_pass, precision=lax.Precision.HIGHEST)
    return (second_pass * sign_f * (maximum / (127.0 * length))).astype(jnp.bfloat16)


def reference(gradients, sign_flips):
    workers = gradients.reshape(N_OUTER * N_DP, BLOCKS, PASS, PASS)
    hadamard_mat = hadamard(PASS)
    sign_f = sign_flips.astype(jnp.float32)

    def max_step(carry, worker_blocks):
        rotated = rotate(worker_blocks.astype(jnp.float32), sign_f, hadamard_mat)
        return jnp.maximum(carry, jnp.max(jnp.abs(rotated))), None

    maximum, _ = lax.scan(max_step, jnp.zeros((), jnp.float32), workers)

    def code_step(carry, worker_blocks):
        rotated = rotate(worker_blocks.astype(jnp.float32), sign_f, hadamard_mat)
        code_vals = quantize(rotated, maximum)
        return carry + code_vals.astype(jnp.float32), None

    code_total, _ = lax.scan(code_step, jnp.zeros((BLOCKS, PASS, PASS), jnp.float32), workers)
    mean_code = code_total / float(N_OUTER * N_DP)
    gradient_sum = decode(code_total, sign_f, hadamard_mat, maximum)
    return mean_code, gradient_sum
```

```python
import functools

import jax
import jax.numpy as jnp
from jax import lax
from jax.experimental import pallas as pl
from jax.experimental.pallas import tpu as pltpu
from jax.sharding import PartitionSpec as P

AXES = ("outer", "dp")
NX, NY, NZ, NC = 4, 4, 8, 2
PASS = 128
HALF = PASS // 2
VMEM = 48 * 1024 * 1024


def coords(index):
    outer, dp = divmod(index, 64)
    return (outer // 2) * 4 + dp // 4 % 4, dp // 16, dp % 4, outer % 2


def linear(z, y, x, c):
    return ((z // 4) * 2 + c) * 64 + (y * 4 + z % 4) * 4 + x


def swap(array, z=0, y=0, x=0, c=0):
    pairs = []
    for index in range(256):
        at = coords(index)
        pairs.append((index, linear(at[0] ^ z, at[1] ^ y, at[2] ^ x, at[3] ^ c)))
    return lax.ppermute(array, AXES, pairs)


def hadamard(length):
    index_row = jnp.arange(length, dtype=jnp.int32)[:, None]
    index_col = jnp.arange(length, dtype=jnp.int32)[None, :]
    common_bits = index_row & index_col
    parity = jnp.zeros((length, length), jnp.int32)
    for bit_pos in range(length.bit_length() - 1):
        parity = parity + (common_bits >> bit_pos & 1)
    return (1 - 2 * (parity % 2)).astype(jnp.float32)


def split3(value):
    high = value.astype(jnp.bfloat16)
    rest = value - high.astype(jnp.float32)
    mid = rest.astype(jnp.bfloat16)
    low = (rest - mid.astype(jnp.float32)).astype(jnp.bfloat16)
    return high, mid, low


def dot(a, b):
    return jnp.dot(a, b, preferred_element_type=jnp.float32)


def params():
    return pltpu.CompilerParams(vmem_limit_bytes=VMEM)


def cost(flops, nbytes):
    return pl.CostEstimate(flops=flops, bytes_accessed=nbytes, transcendentals=0)


STEP = 8


def rotate_kernel(at_ref, x_ref, sign_ref, h_ref, out_ref, max_ref):
    h = h_ref[...]
    flipped = x_ref[...] * sign_ref[...][None]
    first = dot(flipped.reshape(STEP * PASS, PASS), h)
    high, mid, low = split3(first)
    peak = jnp.zeros((8, PASS), jnp.float32)
    for b in range(STEP):
        rows = slice(b * PASS, (b + 1) * PASS)
        turned = (dot(h, high[rows]) + (dot(h, mid[rows]) + dot(h, low[rows]))) * (1.0 / PASS)
        out_ref[b] = turned
        peak = jnp.maximum(peak, jnp.max(jnp.abs(turned).reshape(16, 8, PASS), axis=0))

    @pl.when(pl.program_id(0) == 0)
    def _():
        max_ref[...] = jnp.zeros_like(max_ref)

    max_ref[...] = jnp.maximum(max_ref[...], peak)


def rotate(blocks, at, sign, h):
    steps = 128 // STEP
    return pl.pallas_call(
        rotate_kernel,
        grid_spec=pltpu.PrefetchScalarGridSpec(
            num_scalar_prefetch=1,
            grid=(steps,),
            in_specs=[
                pl.BlockSpec((STEP, PASS, PASS), lambda i, at: (at[0] * steps + i, 0, 0)),
                pl.BlockSpec((PASS, PASS), lambda i, at: (0, 0)),
                pl.BlockSpec((PASS, PASS), lambda i, at: (0, 0)),
            ],
            out_specs=[
                pl.BlockSpec((STEP, PASS, PASS), lambda i, at: (i, 0, 0)),
                pl.BlockSpec((8, PASS), lambda i, at: (0, 0)),
            ],
        ),
        out_shape=[
            jax.ShapeDtypeStruct((128, PASS, PASS), jnp.float32),
            jax.ShapeDtypeStruct((8, PASS), jnp.float32),
        ],
        compiler_params=params(),
        cost_estimate=cost(8 * 128 * PASS**3, 12 << 20),
        name="rotate",
    )(at, blocks, sign, h)


def quantize_kernel(at_ref, max_ref, own_ref, mate_ref, *outs):
    scale = 127.0 / jnp.max(max_ref[...])
    my_y, my_x = at_ref[1], at_ref[2]
    for ky in range(NY):
        for kx in range(NX):
            b = (ky ^ my_y) * NX + (kx ^ my_x)
            code = jnp.floor(own_ref[b] * scale + 0.5) + jnp.floor(mate_ref[b] * scale + 0.5)
            code = code.astype(jnp.bfloat16)
            outs[kx][ky, 0] = code[:HALF]
            outs[NX + ky][kx, 0] = code[HALF:]


def quantize(maximum, own, mate, at):
    piece = jax.ShapeDtypeStruct((4, NZ, HALF, PASS), jnp.bfloat16)
    blocks = pl.BlockSpec((NY * NX, PASS, PASS), lambda i, at: (i ^ at[0], 0, 0))
    return pl.pallas_call(
        quantize_kernel,
        grid_spec=pltpu.PrefetchScalarGridSpec(
            num_scalar_prefetch=1,
            grid=(NZ,),
            in_specs=[pl.BlockSpec((8, PASS), lambda i, at: (0, 0)), blocks, blocks],
            out_specs=[pl.BlockSpec((4, 1, HALF, PASS), lambda i, at: (0, i, 0, 0))] * 8,
        ),
        out_shape=[piece] * 8,
        compiler_params=params(),
        cost_estimate=cost(1 << 24, 20 << 20),
        name="quantize",
    )(at, maximum, own, mate)


def add_first_kernel(*refs):
    total = refs[0][...].astype(jnp.float32)
    for ref in refs[1:4]:
        total = total + ref[...].astype(jnp.float32)
    total = total.astype(jnp.int32).astype(jnp.int16)
    for k in range(4):
        refs[4 + k][...] = total[k]


def add_first(pieces):
    return pl.pallas_call(
        add_first_kernel,
        grid=(2,),
        in_specs=[pl.BlockSpec((4, NZ // 2, HALF, PASS), lambda i: (0, i, 0, 0))] * 4,
        out_specs=[pl.BlockSpec((NZ // 2, HALF, PASS), lambda i: (i, 0, 0))] * 4,
        out_shape=[jax.ShapeDtypeStruct((NZ, HALF, PASS), jnp.int16)] * 4,
        compiler_params=params(),
        cost_estimate=cost(1 << 20, 5 << 19),
        name="add_first",
    )(*pieces)


def add_second_kernel(*refs):
    for half in range(2):
        terms = refs[4 * half : 4 * half + 4]
        total = terms[0][...].astype(jnp.int32)
        for ref in terms[1:]:
            total = total + ref[...].astype(jnp.int32)
        total = total.astype(jnp.int16)
        for k in range(NZ):
            refs[8 + k][half * HALF : (half + 1) * HALF] = total[k]


def add_second(top, bottom):
    return pl.pallas_call(
        add_second_kernel,
        out_shape=[jax.ShapeDtypeStruct((PASS, PASS), jnp.int16)] * NZ,
        compiler_params=params(),
        cost_estimate=cost(1 << 19, 5 << 18),
        name="add_second",
    )(*top, *bottom)


def decode_kernel(*refs):
    max_ref, sign_ref, h_ref = refs[:3]
    terms = refs[3 : 3 + NZ]
    total_ref, out_ref = refs[3 + NZ :]
    total = terms[0][...].astype(jnp.int32)
    for ref in terms[1:]:
        total = total + ref[...].astype(jnp.int32)
    total = total.astype(jnp.float32)
    total_ref[...] = total
    h = h_ref[...]
    high, mid, low = split3(total)
    first = dot(high, h) + (dot(mid, h) + dot(low, h))
    high, mid, low = split3(first)
    second = dot(h, high) + (dot(h, mid) + dot(h, low))
    unit = jnp.max(max_ref[...]) / (127.0 * PASS)
    out_ref[...] = (second * sign_ref[...].astype(jnp.float32) * unit).astype(jnp.bfloat16)


def decode(maximum, sign, h, terms):
    return pl.pallas_call(
        decode_kernel,
        out_shape=[
            jax.ShapeDtypeStruct((PASS, PASS), jnp.float32),
            jax.ShapeDtypeStruct((PASS, PASS), jnp.bfloat16),
        ],
        compiler_params=params(),
        cost_estimate=cost(12 * PASS**3, 1 << 19),
        name="decode",
    )(maximum, sign, h, *terms)


def assemble_kernel(at_ref, *refs):
    pieces, out_ref = refs[:8], refs[-1]
    my_y, my_x = at_ref[1], at_ref[2]
    for ky in range(NY):
        for kx in range(NX):
            b = (ky ^ my_y) * NX + (kx ^ my_x)
            out_ref[b, :HALF] = pieces[kx][ky, 0]
            out_ref[b, HALF:] = pieces[NX + ky][kx, 0]


def assemble(at, pieces, before=None):
    operands = [at, *pieces] + ([] if before is None else [before])
    return pl.pallas_call(
        assemble_kernel,
        grid_spec=pltpu.PrefetchScalarGridSpec(
            num_scalar_prefetch=1,
            grid=(NZ,),
            in_specs=[pl.BlockSpec((4, 1, HALF, PASS), lambda i, at: (0, i, 0, 0))] * 8
            + ([] if before is None else [pl.BlockSpec(memory_space=pl.ANY)]),
            out_specs=pl.BlockSpec((NY * NX, PASS, PASS), lambda i, at: (at[3] * NZ + (i ^ at[0]), 0, 0)),
        ),
        out_shape=jax.ShapeDtypeStruct((256, PASS, PASS), jnp.bfloat16),
        input_output_aliases={} if before is None else {9: 0},
        compiler_params=params(),
        cost_estimate=cost(1 << 10, 8 << 20),
        name="assemble",
    )(*operands)


def xor_order(array, index):
    array = jnp.where(index & 1 == 1, array[jnp.array([1, 0, 3, 2])], array)
    return jnp.where(index & 2 == 2, array[jnp.array([2, 3, 0, 1])], array)


def all_max(value):
    value = jnp.maximum(value, swap(value, c=1))
    for axis, size in (("x", NX), ("y", NY), ("z", NZ)):
        value = functools.reduce(jnp.maximum, [swap(value, **{axis: k}) for k in range(1, size)], value)
    return value


def mean_rows(total, outer, x):
    quarters = xor_order((total / 256.0).reshape(4, PASS // 4, PASS), x)
    got = []
    for r in range(4):
        pairs = []
        for index in range(256):
            z, y, px, c = coords(index)
            pairs.append((index, (px ^ r) * 64 + c * 32 + z * 4 + y))
        got.append(lax.ppermute(quarters[r], AXES, pairs))
    return xor_order(jnp.stack(got), outer)


def body(gradients, sign_flips):
    outer, dp = lax.axis_index("outer"), lax.axis_index("dp")
    z, y, x, c = (outer // 2) * 4 + dp // 4 % 4, dp // 16, dp % 4, outer % 2
    blocks = gradients[0, 0]
    h = hadamard(PASS).astype(jnp.bfloat16)
    sign = sign_flips.astype(jnp.bfloat16)

    def at(core):
        return jnp.stack([z, y, x, core]).astype(jnp.int32)

    mates = swap(lax.dynamic_slice_in_dim(blocks, (1 - c) * 128, 128, 0), c=1)
    own, own_max = rotate(blocks, jnp.stack([c]).astype(jnp.int32), sign, h)
    mate, mate_max = rotate(mates, jnp.zeros((1,), jnp.int32), sign, h)
    maximum = all_max(jnp.maximum(own_max, mate_max))

    pieces = quantize(maximum, own, mate, at(c))
    top, bottom = pieces[:4], pieces[4:]
    top = [top[0]] + [swap(top[k], x=k) for k in range(1, 4)]
    bottom = [bottom[0]] + [swap(bottom[k], y=k) for k in range(1, 4)]
    top, bottom = add_first(top), add_first(bottom)
    top = [top[0]] + [swap(top[k], y=k) for k in range(1, 4)]
    bottom = [bottom[0]] + [swap(bottom[k], x=k) for k in range(1, 4)]
    terms = add_second(top, bottom)
    terms = [terms[0]] + [swap(terms[k], z=k) for k in range(1, NZ)]
    total, decoded = decode(maximum, sign, h, terms)
    mean = mean_rows(total, outer, x)

    line = jnp.stack([decoded] + [swap(decoded, z=k) for k in range(1, NZ)])
    top, bottom = line[:, :HALF], line[:, HALF:]
    top = jnp.stack([top] + [swap(top, y=k) for k in range(1, 4)])
    bottom = jnp.stack([bottom] + [swap(bottom, x=k) for k in range(1, 4)])
    pieces = [top] + [swap(top, x=k) for k in range(1, 4)]
    pieces += [bottom] + [swap(bottom, y=k) for k in range(1, 4)]
    mates = [swap(piece, c=1) for piece in pieces]
    gradient_sum = assemble(at(c), pieces)
    gradient_sum = assemble(at(1 - c), mates, gradient_sum)
    return (mean, gradient_sum)


def solution(mesh):
    placed = (P("outer", "dp", None, None, None), P())
    return jax.shard_map(
        body, mesh=mesh, in_specs=placed, out_specs=(P("dp", "outer", None), P()), check_vma=False
    )
```

```python
import functools

import jax
import jax.numpy as jnp
from jax import lax
from jax.experimental import pallas as pl
from jax.experimental.pallas import tpu as pltpu
from jax.sharding import PartitionSpec as P

AXES = ("outer", "dp")
NX, NY, NZ, NC = 4, 4, 8, 2
PASS = 128
VMEM = 16 * 1024 * 1024


def coords(index):
    outer, dp = divmod(index, 64)
    return (outer // 2) * 4 + dp // 4 % 4, dp // 16, dp % 4, outer % 2


def linear(z, y, x, c):
    return ((z // 4) * 2 + c) * 64 + (y * 4 + z % 4) * 4 + x


def swap(array, z=0, y=0, x=0, c=0):
    pairs = []
    for index in range(256):
        at = coords(index)
        pairs.append((index, linear(at[0] ^ z, at[1] ^ y, at[2] ^ x, at[3] ^ c)))
    return lax.ppermute(array, AXES, pairs)


def exchange(array, varies):
    groups = {}
    for index in range(256):
        fixed = tuple(at for at, name in zip(coords(index), "zyxc") if name not in varies)
        groups.setdefault(fixed, []).append(index)
    return lax.all_to_all(array, AXES, 0, 0, tiled=True, axis_index_groups=list(groups.values()))


def hadamard(length):
    index_row = jnp.arange(length, dtype=jnp.int32)[:, None]
    index_col = jnp.arange(length, dtype=jnp.int32)[None, :]
    common_bits = index_row & index_col
    parity = jnp.zeros((length, length), jnp.int32)
    for bit_pos in range(length.bit_length() - 1):
        parity = parity + (common_bits >> bit_pos & 1)
    return (1 - 2 * (parity % 2)).astype(jnp.float32)


def split3(value):
    high = value.astype(jnp.bfloat16)
    rest = value - high.astype(jnp.float32)
    mid = rest.astype(jnp.bfloat16)
    low = (rest - mid.astype(jnp.float32)).astype(jnp.bfloat16)
    return high, mid, low


def dot(a, b):
    return jnp.dot(a, b, preferred_element_type=jnp.float32)


def params():
    return pltpu.CompilerParams(vmem_limit_bytes=VMEM)


def cost(flops, nbytes):
    return pl.CostEstimate(flops=flops, bytes_accessed=nbytes, transcendentals=0)


def rotate_kernel(core_ref, x_ref, sign_ref, h_ref, out_ref, max_ref):
    h = h_ref[...]
    sign = sign_ref[...]
    peak = jnp.zeros((8, PASS), jnp.float32)
    flipped = [x_ref[0, z % 4, 0, z // 4, 0] * sign for z in range(NZ)]
    first = dot(jnp.concatenate(flipped, axis=0), h)
    high, mid, low = split3(first)
    for z in range(NZ):
        rows = slice(z * PASS, (z + 1) * PASS)
        turned = (dot(h, high[rows]) + (dot(h, mid[rows]) + dot(h, low[rows]))) * (1.0 / PASS)
        out_ref[z] = turned
        peak = jnp.maximum(peak, jnp.max(jnp.abs(turned).reshape(16, 8, PASS), axis=0))

    @pl.when((pl.program_id(0) == 0) & (pl.program_id(1) == 0))
    def _():
        max_ref[...] = jnp.zeros_like(max_ref)

    max_ref[...] = jnp.maximum(max_ref[...], peak)


def bucket_spec(core):
    return pl.BlockSpec((1, 4, 1, 2, 1, PASS, PASS), lambda y, x, at: (y, 0, x, 0, core(at), 0, 0))


def rotate(blocks, core, sign, h):
    return pl.pallas_call(
        rotate_kernel,
        grid_spec=pltpu.PrefetchScalarGridSpec(
            num_scalar_prefetch=1,
            grid=(NY, NX),
            in_specs=[
                bucket_spec(lambda at: at[0]),
                pl.BlockSpec((PASS, PASS), lambda y, x, at: (0, 0)),
                pl.BlockSpec((PASS, PASS), lambda y, x, at: (0, 0)),
            ],
            out_specs=[
                pl.BlockSpec((NZ, PASS, PASS), lambda y, x, at: (y * NX + x, 0, 0)),
                pl.BlockSpec((8, PASS), lambda y, x, at: (0, 0)),
            ],
        ),
        out_shape=[
            pltpu.VMEM((128, PASS, PASS), jnp.float32),
            jax.ShapeDtypeStruct((8, PASS), jnp.float32),
        ],
        compiler_params=params(),
        cost_estimate=cost(8 * 128 * PASS**3, 12 << 20),
        name="rotate",
    )(core, blocks, sign, h)


GROUPS = 4


def hops(group):
    return ("x", "y") if group < 2 else ("y", "x"), (1, 3) if group % 2 == 0 else (3, 1)


def orders(group, y, x):
    axes, (a, b) = hops(group)
    at = {"y": y, "x": x}
    first = at[axes[0]] ^ jnp.array([a, 2, 0, b], jnp.int32)
    second = at[axes[1]] ^ jnp.array([0, b, a, 2], jnp.int32)
    return jnp.concatenate([first, second])


def quantize_kernel(group, at_ref, max_ref, own_ref, mate_ref, sent_ref, kept_ref):
    scale = 127.0 / jnp.max(max_ref[...])

    for out_ref, start in ((sent_ref, 0), (kept_ref, 2)):
        for i in range(2):
            for j in range(4):
                first, second = at_ref[group, start + i], at_ref[group, 4 + j]
                y, x = (second, first) if group < 2 else (first, second)
                for k in range(2):
                    b = (y * NX + x) * NZ + 2 * group + k
                    code = jnp.floor(own_ref[b] * scale + 0.5) + jnp.floor(mate_ref[b] * scale + 0.5)
                    out_ref[i, j, k] = code.astype(jnp.bfloat16)


def in_vmem(array):
    return pltpu.with_memory_space_constraint(array, pltpu.VMEM)


def quantize(group, table, maximum, own, mate):
    vmem = pl.BlockSpec(memory_space=pltpu.VMEM)
    return pl.pallas_call(
        functools.partial(quantize_kernel, group),
        in_specs=[pl.BlockSpec(memory_space=pltpu.SMEM), vmem, vmem, vmem],
        out_specs=[vmem, vmem],
        out_shape=[jax.ShapeDtypeStruct((2, 4, 2, PASS, PASS), jnp.bfloat16)] * 2,
        compiler_params=params(),
        cost_estimate=cost(1 << 22, 5 << 20),
        name="quantize",
    )(table, maximum, own, mate)


def add_kernel(kept_ref, got_ref, low_ref, high_ref):
    count = low_ref.shape[0]
    halves = ((0, low_ref), (count, high_ref)) if len(kept_ref.shape) == len(low_ref.shape) else ((0, low_ref), (1, high_ref))
    for start, out_ref in halves:
        at = pl.ds(start, count) if len(kept_ref.shape) == len(low_ref.shape) else start
        total = kept_ref[at].astype(jnp.int32) + got_ref[at].astype(jnp.int32)
        out_ref[...] = total.astype(jnp.int16)


def add_two(kept, got, shape):
    return pl.pallas_call(
        add_kernel,
        out_shape=[jax.ShapeDtypeStruct(shape, jnp.int16)] * 2,
        compiler_params=params(),
        cost_estimate=cost(kept.size, kept.size * 6),
        name="add_two",
    )(kept, got)


def add_last_kernel(*refs):
    for g in range(GROUPS):
        total = refs[2 * g][...].astype(jnp.int32) + refs[2 * g + 1][...].astype(jnp.int32)
        refs[-1][2 * g : 2 * g + 2] = total.astype(jnp.int16)


def add_last(terms):
    return pl.pallas_call(
        add_last_kernel,
        out_shape=jax.ShapeDtypeStruct((NZ, PASS, PASS), jnp.int16),
        compiler_params=params(),
        cost_estimate=cost(1 << 18, 3 << 18),
        name="add_last",
    )(*terms)


def reduce_plane(table, maximum, own, mate):
    parts = [quantize(g, table, maximum, own, mate) for g in range(GROUPS)]
    for axis in range(2):
        for hop in range(2):
            got = []
            for g in range(GROUPS):
                axes, xors = hops(g)
                got.append(swap(parts[g][0], **{axes[axis]: xors[hop]}))
            if axis == 1 and hop == 1:
                return add_last([t for g in range(GROUPS) for t in (parts[g][1], got[g])])
            if hop == 0:
                shape = parts[0][1].shape[1:]
                parts = [add_two(parts[g][1], got[g], shape)[::-1] for g in range(GROUPS)]
            else:
                shape = (2, *parts[0][1].shape[1:])
                parts = [add_two(parts[g][1], got[g], shape)[::-1] for g in range(GROUPS)]


def gather_plane(line):
    held = [line[2 * g : 2 * g + 2][None] for g in range(GROUPS)]
    for axis in (1, 0):
        for hop in (1, 0):
            got = []
            for g in range(GROUPS):
                axes, xors = hops(g)
                got.append(swap(held[g], **{axes[axis]: xors[hop]}))
            if axis == 0 and hop == 0:
                return [pair for g in range(GROUPS) for pair in (held[g], got[g])]
            held = [jnp.concatenate([held[g], got[g]], axis=0) for g in range(GROUPS)]
        held = [h[None] for h in held]


def assemble_kernel(*refs):
    at_ref, pieces, out_ref, sems = refs[0], refs[1:9], refs[-2], refs[-1]
    copies = []
    for g in range(GROUPS):
        for part in range(2):
            for i in range(2):
                for j in range(4):
                    first = at_ref[g, 2 + i if part == 0 else i]
                    second = at_ref[g, 4 + j]
                    y, x = (second, first) if g < 2 else (first, second)
                    z = 2 * g
                    copies.append(
                        pltpu.make_async_copy(
                            pieces[2 * g + part].at[i, j],
                            out_ref.at[y, pl.ds(z % 4, 2), x, z // 4, at_ref[GROUPS, 0]],
                            sems.at[len(copies)],
                        )
                    )
    for copy in copies:
        copy.start()
    for copy in copies:
        copy.wait()


def assemble(at, pieces, before=None):
    more = [] if before is None else [before]
    anywhere = pl.BlockSpec(memory_space=pl.ANY)
    return pl.pallas_call(
        assemble_kernel,
        in_specs=[pl.BlockSpec(memory_space=pltpu.SMEM)]
        + [pl.BlockSpec(memory_space=pltpu.VMEM)] * 8
        + [anywhere] * len(more),
        out_specs=anywhere,
        out_shape=jax.ShapeDtypeStruct((NY, 4, NX, 2, NC, PASS, PASS), jnp.bfloat16),
        scratch_shapes=[pltpu.SemaphoreType.DMA((64,))],
        input_output_aliases={9: 0} if more else {},
        compiler_params=params(),
        cost_estimate=cost(1 << 10, 8 << 20),
        name="assemble",
    )(at, *pieces, *more)


def all_max(value):
    value = jnp.max(exchange(jnp.broadcast_to(value[None], (NZ * NC, *value.shape)), "zc"), axis=0)
    return jnp.max(exchange(jnp.broadcast_to(value[None], (NY * NX, *value.shape)), "yx"), axis=0)


def decode_kernel(max_ref, sign_ref, h_ref, terms_ref, total_ref, out_ref):
    total = terms_ref[0].astype(jnp.int32)
    for k in range(1, NZ):
        total = total + terms_ref[k].astype(jnp.int32)
    total = total.astype(jnp.float32)
    total_ref[...] = total
    h = h_ref[...]
    high, mid, low = split3(total)
    first = dot(high, h) + (dot(mid, h) + dot(low, h))
    high, mid, low = split3(first)
    second = dot(h, high) + (dot(h, mid) + dot(h, low))
    unit = jnp.max(max_ref[...]) / (127.0 * PASS)
    decoded = (second * sign_ref[...].astype(jnp.float32) * unit).astype(jnp.bfloat16)
    for k in range(NZ):
        out_ref[k] = decoded


def decode(maximum, sign, h, terms):
    return pl.pallas_call(
        decode_kernel,
        out_shape=[
            jax.ShapeDtypeStruct((PASS, PASS), jnp.float32),
            jax.ShapeDtypeStruct((NZ, PASS, PASS), jnp.bfloat16),
        ],
        compiler_params=params(),
        cost_estimate=cost(12 * PASS**3, 1 << 19),
        name="decode",
    )(maximum, sign, h, terms)


def pick(pair, index):
    return jnp.where(index == 0, pair[0], pair[1])


def mean_rows(total, z_high, c):
    rows = (total / 256.0).reshape(2, 2, PASS // 4, PASS)
    kept, sent = pick(rows, z_high), pick(rows, 1 - z_high)
    got = swap(sent, z=4)
    both = jnp.where(z_high == 0, jnp.stack([kept, got]), jnp.stack([got, kept]))
    both = jnp.swapaxes(both, 0, 1)
    kept, sent = pick(both, c), pick(both, 1 - c)
    got = swap(sent, c=1)
    both = jnp.where(c == 0, jnp.stack([kept, got], axis=1), jnp.stack([got, kept], axis=1))
    return both.reshape(4, PASS // 4, PASS)


def body(gradients, sign_flips):
    outer, dp = lax.axis_index("outer"), lax.axis_index("dp")
    z_high, c = outer // 2, outer % 2
    y, x = dp // 16, dp % 4
    bucket = gradients.reshape(NY, 4, NX, 2, NC, PASS, PASS)
    h = hadamard(PASS).astype(jnp.bfloat16)
    sign = sign_flips.astype(jnp.bfloat16)
    here = jnp.stack([c]).astype(jnp.int32)

    mates = swap(lax.dynamic_slice_in_dim(bucket, 1 - c, 1, 4), c=1)
    own, own_max = rotate(bucket, here, sign, h)
    mate, mate_max = rotate(mates, jnp.zeros((1,), jnp.int32), sign, h)
    maximum = all_max(jnp.maximum(own_max, mate_max))

    table = jnp.stack([orders(g, y, x) for g in range(GROUPS)])
    terms = exchange(reduce_plane(table, maximum, in_vmem(own), in_vmem(mate)), "z")
    total, decoded = decode(maximum, sign, h, terms)
    mean = mean_rows(total, z_high, c)

    pieces = gather_plane(exchange(decoded, "z"))
    mates = [swap(piece, c=1) for piece in pieces]
    gradient_sum = assemble(jnp.concatenate([table, jnp.full((1, 8), c, jnp.int32)]), pieces)
    gradient_sum = assemble(jnp.concatenate([table, jnp.full((1, 8), 1 - c, jnp.int32)]), mates, gradient_sum)
    return (mean, gradient_sum.reshape(256, PASS, PASS))


def solution(mesh):
    placed = (P("outer", "dp", None, None, None), P())
    return jax.shard_map(
        body, mesh=mesh, in_specs=placed, out_specs=(P("dp", "outer", None), P()), check_vma=False
    )
```

```python
import functools

import jax
import jax.numpy as jnp
from jax import lax
from jax.experimental import pallas as pl
from jax.experimental.pallas import tpu as pltpu
from jax.sharding import PartitionSpec as P

AXES = ("outer", "dp")
NX, NY, NZ, NC = 4, 4, 8, 2
PASS = 128
VMEM = 16 * 1024 * 1024
HALF = PASS // 2


def coords(index):
    outer, dp = divmod(index, 64)
    return (outer // 2) * 4 + dp // 4 % 4, dp // 16, dp % 4, outer % 2


def linear(z, y, x, c):
    return ((z // 4) * 2 + c) * 64 + (y * 4 + z % 4) * 4 + x


def swap(array, z=0, y=0, x=0, c=0):
    pairs = []
    for index in range(256):
        at = coords(index)
        pairs.append((index, linear(at[0] ^ z, at[1] ^ y, at[2] ^ x, at[3] ^ c)))
    return lax.ppermute(array, AXES, pairs)


def exchange(array, varies):
    groups = {}
    for index in range(256):
        fixed = tuple(at for at, name in zip(coords(index), "zyxc") if name not in varies)
        groups.setdefault(fixed, []).append(index)
    return lax.all_to_all(array, AXES, 0, 0, tiled=True, axis_index_groups=list(groups.values()))


def shift_z(array, step):
    pairs = []
    for index in range(256):
        z, y, x, c = coords(index)
        pairs.append((index, linear((z + step) % NZ, y, x, c)))
    return lax.ppermute(array, AXES, pairs)


def hadamard(length):
    index_row = jnp.arange(length, dtype=jnp.int32)[:, None]
    index_col = jnp.arange(length, dtype=jnp.int32)[None, :]
    common_bits = index_row & index_col
    parity = jnp.zeros((length, length), jnp.int32)
    for bit_pos in range(length.bit_length() - 1):
        parity = parity + (common_bits >> bit_pos & 1)
    return (1 - 2 * (parity % 2)).astype(jnp.float32)


def split3(value):
    high = value.astype(jnp.bfloat16)
    rest = value - high.astype(jnp.float32)
    mid = rest.astype(jnp.bfloat16)
    low = (rest - mid.astype(jnp.float32)).astype(jnp.bfloat16)
    return high, mid, low


def dot(a, b):
    return jnp.dot(a, b, preferred_element_type=jnp.float32)


def params():
    return pltpu.CompilerParams(vmem_limit_bytes=VMEM)


def cost(flops, nbytes):
    return pl.CostEstimate(flops=flops, bytes_accessed=nbytes, transcendentals=0)


def rotate_blocks(blocks, places, sign, wide_h, tall_h, max_ref):
    wide = []
    for block in blocks:
        block = block * sign
        wide.append(jnp.concatenate([block[:HALF], block[HALF:]], axis=1))
    terms = split3(dot(jnp.concatenate(wide, axis=0), wide_h))
    peak = jnp.zeros((8, PASS), jnp.float32)
    for k, (out_ref, at) in enumerate(places):
        rows = slice(k * HALF, (k + 1) * HALF)
        turned = dot(tall_h, jnp.concatenate([term[rows] for term in terms], axis=0))
        for half in range(2):
            part = turned[:, half * PASS : (half + 1) * PASS]
            out_ref[at, half * HALF : (half + 1) * HALF] = part
            peak = jnp.maximum(peak, jnp.max(jnp.abs(part).reshape(8, 8, PASS), axis=0))
    max_ref[...] = jnp.maximum(max_ref[...], peak)


def rotate_own_kernel(core_ref, bucket_ref, sign_ref, wide_ref, tall_ref, low_ref, high_ref, max_ref, held, sems):
    copies = [
        pltpu.make_async_copy(bucket_ref.at[y, :, :, :, core_ref[0]], held.at[y], sems.at[y]) for y in range(NY)
    ]
    for copy in copies:
        copy.start()
    sign, wide_h, tall_h = sign_ref[...], wide_ref[...], tall_ref[...]
    max_ref[...] = jnp.zeros_like(max_ref)
    for y in range(NY):
        copies[y].wait()

        @pl.loop(0, NX // 2)
        def _(pair):
            blocks, places = [], []
            for k in range(16):
                x, high, z = pair * 2 + k // 8, k // 4 % 2, k % 4
                blocks.append(held[y, z, x, high])
                places.append(((low_ref, high_ref)[high], (y * NX + x) * 4 + z))
            rotate_blocks(blocks, places, sign, wide_h, tall_h, max_ref)


def rotate_own(core, bucket, sign, wide_h, tall_h):
    vmem = pl.BlockSpec(memory_space=pltpu.VMEM)
    return pl.pallas_call(
        rotate_own_kernel,
        in_specs=[pl.BlockSpec(memory_space=pltpu.SMEM), pl.BlockSpec(memory_space=pl.ANY), vmem, vmem, vmem],
        out_specs=[vmem] * 3,
        out_shape=[pltpu.VMEM((64, PASS, PASS), jnp.float32)] * 2 + [pltpu.VMEM((8, PASS), jnp.float32)],
        scratch_shapes=[pltpu.VMEM((NY, 4, NX, 2, PASS, PASS), jnp.bfloat16), pltpu.SemaphoreType.DMA((NY,))],
        compiler_params=params(),
        cost_estimate=cost(8 * 128 * PASS**3, 12 << 20),
        name="rotate_own",
    )(core, bucket, sign, wide_h, tall_h)


def rotate_mate_kernel(half_ref, before_ref, sign_ref, wide_ref, tall_ref, out_ref, max_ref):
    sign, wide_h, tall_h = sign_ref[...], wide_ref[...], tall_ref[...]
    max_ref[...] = before_ref[...]

    for y in range(NY):
        blocks = [half_ref[y, k % 4, k // 4] for k in range(16)]
        rotate_blocks(blocks, [(out_ref, y * 16 + k) for k in range(16)], sign, wide_h, tall_h, max_ref)


def rotate_mate(half, before, sign, wide_h, tall_h):
    vmem = pl.BlockSpec(memory_space=pltpu.VMEM)
    return pl.pallas_call(
        rotate_mate_kernel,
        in_specs=[vmem] * 5,
        out_specs=[vmem] * 2,
        out_shape=[pltpu.VMEM((64, PASS, PASS), jnp.float32), pltpu.VMEM((8, PASS), jnp.float32)],
        compiler_params=params(),
        cost_estimate=cost(4 * 128 * PASS**3, 6 << 20),
        name="rotate_mate",
    )(half, before, sign, wide_h, tall_h)


def cut_kernel(core_ref, bucket_ref, low_ref, high_ref, sems):
    copies = []
    for high, out_ref in enumerate((low_ref, high_ref)):
        for y in range(NY):
            source = bucket_ref.at[y, :, :, high, core_ref[0]]
            copies.append(pltpu.make_async_copy(source, out_ref.at[y], sems.at[len(copies)]))
    for copy in copies:
        copy.start()
    for copy in copies:
        copy.wait()


def cut(core, bucket):
    vmem = pl.BlockSpec(memory_space=pltpu.VMEM)
    return pl.pallas_call(
        cut_kernel,
        in_specs=[pl.BlockSpec(memory_space=pltpu.SMEM), pl.BlockSpec(memory_space=pl.ANY)],
        out_specs=[vmem] * 2,
        out_shape=[jax.ShapeDtypeStruct((NY, 4, NX, PASS, PASS), jnp.bfloat16)] * 2,
        scratch_shapes=[pltpu.SemaphoreType.DMA((2 * NY,))],
        compiler_params=params(),
        cost_estimate=cost(1 << 10, 8 << 20),
        name="cut",
    )(core, bucket)


def max_kernel(*refs):
    value = refs[0][...]
    for ref in refs[1:-1]:
        value = jnp.maximum(value, ref[...])
    refs[-1][...] = value


def max_of(*values):
    return pl.pallas_call(
        max_kernel,
        out_shape=jax.ShapeDtypeStruct((8, PASS), jnp.float32),
        compiler_params=params(),
        name="max_of",
    )(*values)


def all_max(value):
    value = max_of(value, swap(value, c=1))
    for xor in (1, 3):
        value = max_of(value, swap(value, x=xor), swap(value, y=xor), swap(value, x=xor, y=xor))
    for step in (1, 3):
        value = max_of(value, shift_z(value, step), shift_z(value, -step))
    return value


GROUPS = 4


def hops(group):
    return "x" if group < 2 else "y", (1, 3) if group % 2 == 0 else (3, 1)


def orders(group, y, x):
    _, (a, b) = hops(group)
    mine, other = (x, y) if group < 2 else (y, x)
    return jnp.concatenate([mine ^ jnp.array([a, 2, 0, b], jnp.int32), other ^ jnp.array([0, 1, 2, 3], jnp.int32)])


def quantize_kernel(group, at_ref, max_ref, own_ref, mate_ref, sent_ref, kept_ref):
    scale = 127.0 / jnp.max(max_ref[...])

    for out_ref, start in ((sent_ref, 0), (kept_ref, 2)):
        for i in range(2):
            for j in range(4):
                first, second = at_ref[group, start + i], at_ref[group, 4 + j]
                y, x = (second, first) if group < 2 else (first, second)
                for k in range(2):
                    b = (y * NX + x) * 4 + 2 * group % 4 + k
                    code = jnp.floor(own_ref[b] * scale + 0.5) + jnp.floor(mate_ref[b] * scale + 0.5)
                    out_ref[i, j, k] = code.astype(jnp.bfloat16)


def in_vmem(array):
    return pltpu.with_memory_space_constraint(array, pltpu.VMEM)


def quantize(group, table, maximum, own, mate):
    vmem = pl.BlockSpec(memory_space=pltpu.VMEM)
    return pl.pallas_call(
        functools.partial(quantize_kernel, group),
        in_specs=[pl.BlockSpec(memory_space=pltpu.SMEM), vmem, vmem, vmem],
        out_specs=[vmem, vmem],
        out_shape=[jax.ShapeDtypeStruct((2, 4, 2, PASS, PASS), jnp.bfloat16)] * 2,
        compiler_params=params(),
        cost_estimate=cost(1 << 22, 5 << 20),
        name="quantize",
    )(table, maximum, own, mate)


def add_first_kernel(kept_ref, got_ref, low_ref, high_ref):
    for start, out_ref in ((0, low_ref), (1, high_ref)):
        total = kept_ref[start].astype(jnp.int32) + got_ref[start].astype(jnp.int32)
        out_ref[...] = total.astype(jnp.int16)


def add_first(kept, got):
    return pl.pallas_call(
        add_first_kernel,
        out_shape=[jax.ShapeDtypeStruct(kept.shape[1:], jnp.int16)] * 2,
        compiler_params=params(),
        cost_estimate=cost(kept.size, kept.size * 6),
        name="add_first",
    )(kept, got)


def add_pair_kernel(*refs):
    for g in range(2):
        total = refs[2 * g][...].astype(jnp.int32) + refs[2 * g + 1][...].astype(jnp.int32)
        total = total.astype(jnp.int16)
        for k in range(4):
            refs[4 + k][2 * g : 2 * g + 2] = total[k]


def add_pair(terms):
    return pl.pallas_call(
        add_pair_kernel,
        out_shape=[jax.ShapeDtypeStruct((4, PASS, PASS), jnp.int16)] * 4,
        compiler_params=params(),
        cost_estimate=cost(1 << 19, 3 << 19),
        name="add_pair",
    )(*terms)


def add_last_kernel(*refs):
    for pair in range(2):
        total = refs[4 * pair][...].astype(jnp.int32)
        for k in range(1, 4):
            total = total + refs[4 * pair + k][...].astype(jnp.int32)
        refs[-1][4 * pair : 4 * pair + 4] = total.astype(jnp.int16)


def add_last(terms):
    return pl.pallas_call(
        add_last_kernel,
        out_shape=jax.ShapeDtypeStruct((NZ, PASS, PASS), jnp.int16),
        compiler_params=params(),
        cost_estimate=cost(1 << 18, 3 << 18),
        name="add_last",
    )(*terms)


def spread(array, axis):
    return [swap(array[k] if isinstance(array, (list, tuple)) else array, **{axis: k}) for k in range(1, 4)]


def reduce_plane(table, maximum, own, mate):
    parts = [quantize(g, table, maximum, in_vmem(own[g // 2]), in_vmem(mate[g // 2])) for g in range(GROUPS)]
    for hop in range(2):
        got = []
        for g in range(GROUPS):
            axis, xors = hops(g)
            got.append(swap(parts[g][0], **{axis: xors[hop]}))
        if hop == 0:
            parts = [add_first(parts[g][1], got[g])[::-1] for g in range(GROUPS)]
    terms = []
    for pair, axis in enumerate(("y", "x")):
        cuts = add_pair([t for g in (2 * pair, 2 * pair + 1) for t in (parts[g][1], got[g])])
        terms += [cuts[0], *spread(cuts, axis)]
    return add_last(terms)


def gather_plane(line):
    terms = []
    for pair, axis in enumerate(("y", "x")):
        part = line[4 * pair : 4 * pair + 4]
        terms += [part, *spread(part, axis)]
    held = deal(terms)
    for hop in (1, 0):
        got = []
        for g in range(GROUPS):
            axis, xors = hops(g)
            got.append(swap(held[g], **{axis: xors[hop]}))
        if hop == 1:
            held = [jnp.concatenate([held[g], got[g]], axis=0) for g in range(GROUPS)]
    return held, got


def placements(at_ref, start, pieces, out_ref, sems):
    copies = []
    for g in range(GROUPS):
        for i in range(2):
            for j in range(4):
                first, second = at_ref[g, start + i], at_ref[g, 4 + j]
                y, x = (second, first) if g < 2 else (first, second)
                place = out_ref.at[y, pl.ds(2 * g % 4, 2), x, g // 2, at_ref[GROUPS, 0]]
                copies.append(pltpu.make_async_copy(pieces[g].at[i, j], place, sems.at[len(copies)]))
    return copies


def assemble_kernel(start, count, at_ref, *refs):
    pieces, out_ref, sems = refs[:count], refs[-2], refs[-1]
    if count == 1:
        pieces = [pieces[0].at[g] for g in range(GROUPS)]
    copies = placements(at_ref, start, pieces, out_ref, sems)
    for copy in copies:
        copy.start()
    for copy in copies:
        copy.wait()


def assemble(start, at, pieces, before=None):
    more = [] if before is None else [before]
    anywhere = pl.BlockSpec(memory_space=pl.ANY)
    return pl.pallas_call(
        functools.partial(assemble_kernel, start, len(pieces)),
        in_specs=[pl.BlockSpec(memory_space=pltpu.SMEM)]
        + [pl.BlockSpec(memory_space=pltpu.VMEM)] * len(pieces)
        + [anywhere] * len(more),
        out_specs=anywhere,
        out_shape=jax.ShapeDtypeStruct((NY, 4, NX, 2, NC, PASS, PASS), jnp.bfloat16),
        scratch_shapes=[pltpu.SemaphoreType.DMA((8 * GROUPS,))],
        input_output_aliases={1 + len(pieces): 0} if more else {},
        compiler_params=params(),
        cost_estimate=cost(1 << 10, 4 << 20),
        name="assemble",
    )(at, *pieces, *more)


def decode_kernel(max_ref, sign_ref, h_ref, terms_ref, total_ref, out_ref):
    total = terms_ref[0].astype(jnp.int32)
    for k in range(1, NZ):
        total = total + terms_ref[k].astype(jnp.int32)
    total = total.astype(jnp.float32)
    total_ref[...] = total
    h = h_ref[...]
    high, mid, low = split3(total)
    first = dot(high, h) + (dot(mid, h) + dot(low, h))
    high, mid, low = split3(first)
    second = dot(h, high) + (dot(h, mid) + dot(h, low))
    unit = jnp.max(max_ref[...]) / (127.0 * PASS)
    decoded = (second * sign_ref[...].astype(jnp.float32) * unit).astype(jnp.bfloat16)
    for k in range(NZ):
        out_ref[k] = decoded


def decode(maximum, sign, h, terms):
    return pl.pallas_call(
        decode_kernel,
        out_shape=[
            jax.ShapeDtypeStruct((PASS, PASS), jnp.float32),
            jax.ShapeDtypeStruct((NZ, PASS, PASS), jnp.bfloat16),
        ],
        compiler_params=params(),
        cost_estimate=cost(12 * PASS**3, 1 << 19),
        name="decode",
    )(maximum, sign, h, terms)


def deal_kernel(*refs):
    for g in range(GROUPS):
        for k in range(4):
            refs[8 + g][0, k] = refs[g // 2 * 4 + k][2 * (g % 2) : 2 * (g % 2) + 2]


def deal(terms):
    return pl.pallas_call(
        deal_kernel,
        out_shape=[jax.ShapeDtypeStruct((1, 4, 2, PASS, PASS), jnp.bfloat16)] * GROUPS,
        compiler_params=params(),
        cost_estimate=cost(1 << 10, 1 << 21),
        name="deal",
    )(*terms)


def after_kernel(*refs):
    pass


def after(array, before):
    anywhere = pl.BlockSpec(memory_space=pl.ANY)
    return pl.pallas_call(
        after_kernel,
        in_specs=[anywhere] * 2,
        out_specs=[anywhere] * 2,
        out_shape=[jax.ShapeDtypeStruct(a.shape, a.dtype) for a in (array, before)],
        input_output_aliases={0: 0, 1: 1},
        compiler_params=params(),
        name="after",
    )(array, before)


def pick(pair, index):
    return jnp.where(index == 0, pair[0], pair[1])


def mean_rows(kept, got, z_high, c):
    both = jnp.where(z_high == 0, jnp.stack([kept, got], axis=1), jnp.stack([got, kept], axis=1))
    kept, sent = pick(both, c), pick(both, 1 - c)
    got = swap(sent, c=1)
    both = jnp.where(c == 0, jnp.stack([kept, got], axis=1), jnp.stack([got, kept], axis=1))
    return both.reshape(4, PASS // 4, PASS)


def body(gradients, sign_flips):
    outer, dp = lax.axis_index("outer"), lax.axis_index("dp")
    z_high, c = outer // 2, outer % 2
    y, x = dp // 16, dp % 4
    bucket = pltpu.with_memory_space_constraint(gradients.reshape(NY, 4, NX, 2, NC, PASS, PASS), pltpu.HBM)
    h = hadamard(PASS).astype(jnp.bfloat16)
    wide_h = hadamard(2 * PASS).astype(jnp.bfloat16)
    tall_h = jnp.tile(hadamard(HALF) / PASS, (1, 3)).astype(jnp.bfloat16)
    sign = sign_flips.astype(jnp.bfloat16)
    here = jnp.stack([c]).astype(jnp.int32)

    sent = [swap(half, c=1) for half in cut(1 - here, bucket)]
    *own, maximum = rotate_own(here, bucket, sign, wide_h, tall_h)
    mate = []
    for half in sent:
        rotated, maximum = rotate_mate(in_vmem(half), maximum, sign, wide_h, tall_h)
        mate.append(rotated)
    maximum = all_max(maximum)

    table = jnp.stack([orders(g, y, x) for g in range(GROUPS)])
    terms = exchange(reduce_plane(table, maximum, own, mate), "z")
    total, decoded = decode(maximum, sign, h, terms)
    rows = (total / 256.0).reshape(2, 2, PASS // 4, PASS)
    kept, sent = pick(rows, z_high), pick(rows, 1 - z_high)
    line, got = after(exchange(decoded, "z"), swap(sent, z=4))
    mean = mean_rows(kept, got, z_high, c)

    near, far = gather_plane(line)
    own_at = jnp.concatenate([table, jnp.full((1, 8), c, jnp.int32)])
    mate_at = jnp.concatenate([table, jnp.full((1, 8), 1 - c, jnp.int32)])
    near_mates = swap(jnp.stack(near), c=1)
    gradient_sum = assemble(2, own_at, near)
    gradient_sum = assemble(2, mate_at, [near_mates], gradient_sum)
    far_mates = [None] * GROUPS
    for g in (2, 1, 0, 3):
        far[g], gradient_sum = after(far[g], gradient_sum)
        far_mates[g] = swap(far[g], c=1)
    gradient_sum = assemble(0, own_at, far, gradient_sum)
    gradient_sum = assemble(0, mate_at, far_mates, gradient_sum)
    return (mean, gradient_sum.reshape(256, PASS, PASS))


def solution(mesh):
    placed = (P("outer", "dp", None, None, None), P())
    return jax.shard_map(
        body, mesh=mesh, in_specs=placed, out_specs=(P("dp", "outer", None), P()), check_vma=False
    )
```

```python
import functools

import jax
import jax.numpy as jnp
from jax import lax
from jax.experimental import pallas as pl
from jax.experimental.pallas import tpu as pltpu
from jax.sharding import PartitionSpec as P

AXES = ("outer", "dp")
NX, NY, NZ, NC = 4, 4, 8, 2
PASS = 128
VMEM = 16 * 1024 * 1024
HALF = PASS // 2


def coords(index):
    outer, dp = divmod(index, 64)
    return (outer // 2) * 4 + dp // 4 % 4, dp // 16, dp % 4, outer % 2


def linear(z, y, x, c):
    return ((z // 4) * 2 + c) * 64 + (y * 4 + z % 4) * 4 + x


def swap(array, z=0, y=0, x=0, c=0):
    pairs = []
    for index in range(256):
        at = coords(index)
        pairs.append((index, linear(at[0] ^ z, at[1] ^ y, at[2] ^ x, at[3] ^ c)))
    return lax.ppermute(array, AXES, pairs)


def exchange(array, varies):
    groups = {}
    for index in range(256):
        fixed = tuple(at for at, name in zip(coords(index), "zyxc") if name not in varies)
        groups.setdefault(fixed, []).append(index)
    return lax.all_to_all(array, AXES, 0, 0, tiled=True, axis_index_groups=list(groups.values()))


def shift_z(array, step):
    pairs = []
    for index in range(256):
        z, y, x, c = coords(index)
        pairs.append((index, linear((z + step) % NZ, y, x, c)))
    return lax.ppermute(array, AXES, pairs)


def hadamard(length):
    index_row = jnp.arange(length, dtype=jnp.int32)[:, None]
    index_col = jnp.arange(length, dtype=jnp.int32)[None, :]
    common_bits = index_row & index_col
    parity = jnp.zeros((length, length), jnp.int32)
    for bit_pos in range(length.bit_length() - 1):
        parity = parity + (common_bits >> bit_pos & 1)
    return (1 - 2 * (parity % 2)).astype(jnp.float32)


def split3(value):
    high = value.astype(jnp.bfloat16)
    rest = value - high.astype(jnp.float32)
    mid = rest.astype(jnp.bfloat16)
    low = (rest - mid.astype(jnp.float32)).astype(jnp.bfloat16)
    return high, mid, low


def dot(a, b):
    return jnp.dot(a, b, preferred_element_type=jnp.float32)


def params():
    return pltpu.CompilerParams(vmem_limit_bytes=VMEM)


def cost(flops, nbytes):
    return pl.CostEstimate(flops=flops, bytes_accessed=nbytes, transcendentals=0)


def rotate_blocks(blocks, places, sign, wide_h, tall_h, max_ref):
    wide = []
    for block in blocks:
        block = block * sign
        wide.append(jnp.concatenate([block[:HALF], block[HALF:]], axis=1))
    terms = split3(dot(jnp.concatenate(wide, axis=0), wide_h))
    peak = jnp.zeros((8, PASS), jnp.float32)
    for k, (out_ref, at) in enumerate(places):
        rows = slice(k * HALF, (k + 1) * HALF)
        turned = dot(tall_h, jnp.concatenate([term[rows] for term in terms], axis=0))
        for half in range(2):
            part = turned[:, half * PASS : (half + 1) * PASS]
            out_ref[at, half * HALF : (half + 1) * HALF] = part
            peak = jnp.maximum(peak, jnp.max(jnp.abs(part).reshape(8, 8, PASS), axis=0))
    max_ref[...] = jnp.maximum(max_ref[...], peak)


def rotate_own_kernel(core_ref, bucket_ref, sign_ref, wide_ref, tall_ref, low_ref, high_ref, max_ref, held, sems):
    copies = [
        pltpu.make_async_copy(bucket_ref.at[y, :, :, :, core_ref[0]], held.at[y], sems.at[y]) for y in range(NY)
    ]
    for copy in copies:
        copy.start()
    sign, wide_h, tall_h = sign_ref[...], wide_ref[...], tall_ref[...]
    max_ref[...] = jnp.zeros_like(max_ref)
    for y in range(NY):
        copies[y].wait()

        @pl.loop(0, NX // 2)
        def _(pair):
            blocks, places = [], []
            for k in range(16):
                x, high, z = pair * 2 + k // 8, k // 4 % 2, k % 4
                blocks.append(held[y, z, x, high])
                places.append(((low_ref, high_ref)[high], (y * NX + x) * 4 + z))
            rotate_blocks(blocks, places, sign, wide_h, tall_h, max_ref)


def rotate_own(core, bucket, sign, wide_h, tall_h):
    vmem = pl.BlockSpec(memory_space=pltpu.VMEM)
    return pl.pallas_call(
        rotate_own_kernel,
        in_specs=[pl.BlockSpec(memory_space=pltpu.SMEM), pl.BlockSpec(memory_space=pl.ANY), vmem, vmem, vmem],
        out_specs=[vmem] * 3,
        out_shape=[pltpu.VMEM((64, PASS, PASS), jnp.float32)] * 2 + [pltpu.VMEM((8, PASS), jnp.float32)],
        scratch_shapes=[pltpu.VMEM((NY, 4, NX, 2, PASS, PASS), jnp.bfloat16), pltpu.SemaphoreType.DMA((NY,))],
        compiler_params=params(),
        cost_estimate=cost(8 * 128 * PASS**3, 12 << 20),
        name="rotate_own",
    )(core, bucket, sign, wide_h, tall_h)


def rotate_mate_kernel(half_ref, before_ref, sign_ref, wide_ref, tall_ref, out_ref, max_ref):
    sign, wide_h, tall_h = sign_ref[...], wide_ref[...], tall_ref[...]
    max_ref[...] = before_ref[...]

    for y in range(NY):
        blocks = [half_ref[y, k % 4, k // 4] for k in range(16)]
        rotate_blocks(blocks, [(out_ref, y * 16 + k) for k in range(16)], sign, wide_h, tall_h, max_ref)


def rotate_mate(half, before, sign, wide_h, tall_h):
    vmem = pl.BlockSpec(memory_space=pltpu.VMEM)
    return pl.pallas_call(
        rotate_mate_kernel,
        in_specs=[vmem] * 5,
        out_specs=[vmem] * 2,
        out_shape=[pltpu.VMEM((64, PASS, PASS), jnp.float32), pltpu.VMEM((8, PASS), jnp.float32)],
        compiler_params=params(),
        cost_estimate=cost(4 * 128 * PASS**3, 6 << 20),
        name="rotate_mate",
    )(half, before, sign, wide_h, tall_h)


def cut_kernel(core_ref, bucket_ref, low_ref, high_ref, sems):
    copies = []
    for high, out_ref in enumerate((low_ref, high_ref)):
        for y in range(NY):
            source = bucket_ref.at[y, :, :, high, core_ref[0]]
            copies.append(pltpu.make_async_copy(source, out_ref.at[y], sems.at[len(copies)]))
    for copy in copies:
        copy.start()
    for copy in copies:
        copy.wait()


def cut(core, bucket):
    vmem = pl.BlockSpec(memory_space=pltpu.VMEM)
    return pl.pallas_call(
        cut_kernel,
        in_specs=[pl.BlockSpec(memory_space=pltpu.SMEM), pl.BlockSpec(memory_space=pl.ANY)],
        out_specs=[vmem] * 2,
        out_shape=[jax.ShapeDtypeStruct((NY, 4, NX, PASS, PASS), jnp.bfloat16)] * 2,
        scratch_shapes=[pltpu.SemaphoreType.DMA((2 * NY,))],
        compiler_params=params(),
        cost_estimate=cost(1 << 10, 8 << 20),
        name="cut",
    )(core, bucket)


def max_kernel(whole, *refs):
    value = refs[0][...]
    for ref in refs[1:-1]:
        value = jnp.maximum(value, ref[...])
    refs[-1][...] = jnp.full_like(value, jnp.max(value)) if whole else value


def max_of(*values, whole=False):
    return pl.pallas_call(
        functools.partial(max_kernel, whole),
        out_shape=jax.ShapeDtypeStruct((8, PASS), jnp.float32),
        compiler_params=params(),
        name="max_of",
    )(*values)


def all_max(value):
    value = max_of(value, swap(value, c=1))
    for xor in (1, 3):
        value = max_of(value, swap(value, x=xor), swap(value, y=xor), swap(value, x=xor, y=xor))
    for step in (1, 3):
        value = max_of(value, shift_z(value, step), shift_z(value, -step), whole=step == 3)
    return value


GROUPS = 4


def hops(group):
    return "x" if group < 2 else "y", (1, 3) if group % 2 == 0 else (3, 1)


def orders(group, y, x):
    _, (a, b) = hops(group)
    mine, other = (x, y) if group < 2 else (y, x)
    return jnp.concatenate([mine ^ jnp.array([a, 2, 0, b], jnp.int32), other ^ jnp.array([0, 1, 2, 3], jnp.int32)])


def quantize_kernel(group, start, at_ref, max_ref, own_ref, mate_ref, out_ref):
    scale = 127.0 / max_ref[:1]
    for i in range(2):
        for j in range(4):
            first, second = at_ref[group, start + i], at_ref[group, 4 + j]
            y, x = (second, first) if group < 2 else (first, second)
            for k in range(2):
                b = (y * NX + x) * 4 + 2 * group % 4 + k
                code = jnp.floor(own_ref[b] * scale + 0.5) + jnp.floor(mate_ref[b] * scale + 0.5)
                out_ref[i, j, k] = code.astype(jnp.bfloat16)


def in_vmem(array):
    return pltpu.with_memory_space_constraint(array, pltpu.VMEM)


def quantize(group, start, table, maximum, own, mate):
    vmem = pl.BlockSpec(memory_space=pltpu.VMEM)
    return pl.pallas_call(
        functools.partial(quantize_kernel, group, start),
        in_specs=[pl.BlockSpec(memory_space=pltpu.SMEM), vmem, vmem, vmem],
        out_specs=vmem,
        out_shape=jax.ShapeDtypeStruct((2, 4, 2, PASS, PASS), jnp.bfloat16),
        compiler_params=params(),
        cost_estimate=cost(1 << 21, 5 << 19),
        name="quantize",
    )(table, maximum, own, mate)


def add_first_kernel(kept_ref, got_ref, low_ref, high_ref):
    for start, out_ref in ((0, low_ref), (1, high_ref)):
        total = kept_ref[start].astype(jnp.int32) + got_ref[start].astype(jnp.int32)
        out_ref[...] = total.astype(jnp.int16)


def add_first(kept, got):
    return pl.pallas_call(
        add_first_kernel,
        out_shape=[jax.ShapeDtypeStruct(kept.shape[1:], jnp.int16)] * 2,
        compiler_params=params(),
        cost_estimate=cost(kept.size, kept.size * 6),
        name="add_first",
    )(kept, got)


def add_pair_kernel(*refs):
    for g in range(2):
        total = refs[2 * g][...].astype(jnp.int32) + refs[2 * g + 1][...].astype(jnp.int32)
        total = total.astype(jnp.int16)
        for k in range(4):
            refs[4 + k][2 * g : 2 * g + 2] = total[k]


def add_pair(terms):
    return pl.pallas_call(
        add_pair_kernel,
        out_shape=[jax.ShapeDtypeStruct((4, PASS, PASS), jnp.int16)] * 4,
        compiler_params=params(),
        cost_estimate=cost(1 << 19, 3 << 19),
        name="add_pair",
    )(*terms)


def add_last_kernel(*refs):
    for pair in range(2):
        total = refs[4 * pair][...].astype(jnp.int32)
        for k in range(1, 4):
            total = total + refs[4 * pair + k][...].astype(jnp.int32)
        refs[-1][4 * pair : 4 * pair + 4] = total.astype(jnp.int16)


def add_last(terms):
    return pl.pallas_call(
        add_last_kernel,
        out_shape=jax.ShapeDtypeStruct((NZ, PASS, PASS), jnp.int16),
        compiler_params=params(),
        cost_estimate=cost(1 << 18, 3 << 18),
        name="add_last",
    )(*terms)


def spread(array, axis):
    return [swap(array[k] if isinstance(array, (list, tuple)) else array, **{axis: k}) for k in range(1, 4)]


def reduce_plane(table, maximum, own, mate):
    parts = [
        [quantize(g, start, table, maximum, in_vmem(own[g // 2]), in_vmem(mate[g // 2])) for start in (0, 2)]
        for g in range(GROUPS)
    ]
    for hop in range(2):
        got = []
        for g in range(GROUPS):
            axis, xors = hops(g)
            got.append(swap(parts[g][0], **{axis: xors[hop]}))
        if hop == 0:
            parts = [add_first(parts[g][1], got[g])[::-1] for g in range(GROUPS)]
    terms = []
    for pair, axis in enumerate(("y", "x")):
        cuts = add_pair([t for g in (2 * pair, 2 * pair + 1) for t in (parts[g][1], got[g])])
        terms += [cuts[0], *spread(cuts, axis)]
    return add_last(terms)


def gather_plane(line, mean):
    terms = []
    for pair, axis in enumerate(("y", "x")):
        part = line[4 * pair : 4 * pair + 4]
        terms += [part, *spread(part, axis)]
    held = deal(terms)
    for hop in (1, 0):
        got = []
        for g in range(GROUPS):
            axis, xors = hops(g)
            got.append(swap(held[g], **{axis: xors[hop]}))
        if hop == 1:
            got[0], mean = after(got[0], mean)
            held = [jnp.concatenate([held[g], got[g]], axis=0) for g in range(GROUPS)]
    return held, got, mean


def placements(at_ref, start, pieces, out_ref, sems):
    copies = []
    for g in range(GROUPS):
        for i in range(2):
            for j in range(4):
                first, second = at_ref[g, start + i], at_ref[g, 4 + j]
                y, x = (second, first) if g < 2 else (first, second)
                place = out_ref.at[y, pl.ds(2 * g % 4, 2), x, g // 2, at_ref[GROUPS, 0]]
                copies.append(pltpu.make_async_copy(pieces[g].at[i, j], place, sems.at[len(copies)]))
    return copies


def assemble_kernel(start, count, at_ref, *refs):
    pieces, out_ref, sems = refs[:count], refs[-2], refs[-1]
    if count == 1:
        pieces = [pieces[0].at[g] for g in range(GROUPS)]
    copies = placements(at_ref, start, pieces, out_ref, sems)
    for copy in copies:
        copy.start()
    for copy in copies:
        copy.wait()


def assemble(start, at, pieces, before=None):
    more = [] if before is None else [before]
    anywhere = pl.BlockSpec(memory_space=pl.ANY)
    return pl.pallas_call(
        functools.partial(assemble_kernel, start, len(pieces)),
        in_specs=[pl.BlockSpec(memory_space=pltpu.SMEM)]
        + [pl.BlockSpec(memory_space=pltpu.VMEM)] * len(pieces)
        + [anywhere] * len(more),
        out_specs=anywhere,
        out_shape=jax.ShapeDtypeStruct((NY, 4, NX, 2, NC, PASS, PASS), jnp.bfloat16),
        scratch_shapes=[pltpu.SemaphoreType.DMA((8 * GROUPS,))],
        input_output_aliases={1 + len(pieces): 0} if more else {},
        compiler_params=params(),
        cost_estimate=cost(1 << 10, 4 << 20),
        name="assemble",
    )(at, *pieces, *more)


def decode_kernel(max_ref, sign_ref, h_ref, terms_ref, total_ref, out_ref):
    total = terms_ref[0].astype(jnp.int32)
    for k in range(1, NZ):
        total = total + terms_ref[k].astype(jnp.int32)
    total = total.astype(jnp.float32)
    total_ref[...] = total
    h = h_ref[...]
    high, mid, low = split3(total)
    first = dot(high, h) + (dot(mid, h) + dot(low, h))
    high, mid, low = split3(first)
    second = dot(h, high) + (dot(h, mid) + dot(h, low))
    unit = max_ref[:1] / (127.0 * PASS)
    decoded = (second * sign_ref[...].astype(jnp.float32) * unit).astype(jnp.bfloat16)
    for k in range(NZ):
        out_ref[k] = decoded


def decode(maximum, sign, h, terms):
    return pl.pallas_call(
        decode_kernel,
        out_shape=[
            jax.ShapeDtypeStruct((PASS, PASS), jnp.float32),
            jax.ShapeDtypeStruct((NZ, PASS, PASS), jnp.bfloat16),
        ],
        compiler_params=params(),
        cost_estimate=cost(12 * PASS**3, 1 << 19),
        name="decode",
    )(maximum, sign, h, terms)


def deal_kernel(*refs):
    for g in range(GROUPS):
        for k in range(4):
            refs[8 + g][0, k] = refs[g // 2 * 4 + k][2 * (g % 2) : 2 * (g % 2) + 2]


def deal(terms):
    return pl.pallas_call(
        deal_kernel,
        out_shape=[jax.ShapeDtypeStruct((1, 4, 2, PASS, PASS), jnp.bfloat16)] * GROUPS,
        compiler_params=params(),
        cost_estimate=cost(1 << 10, 1 << 21),
        name="deal",
    )(*terms)


def after_kernel(*refs):
    pass


def after(array, before):
    anywhere = pl.BlockSpec(memory_space=pl.ANY)
    return pl.pallas_call(
        after_kernel,
        in_specs=[anywhere] * 2,
        out_specs=[anywhere] * 2,
        out_shape=[jax.ShapeDtypeStruct(a.shape, a.dtype) for a in (array, before)],
        input_output_aliases={0: 0, 1: 1},
        compiler_params=params(),
        name="after",
    )(array, before)


def pick(pair, index):
    return jnp.where(index == 0, pair[0], pair[1])


def mean_rows(kept, got, z_high, c):
    both = jnp.where(z_high == 0, jnp.stack([kept, got], axis=1), jnp.stack([got, kept], axis=1))
    kept, sent = pick(both, c), pick(both, 1 - c)
    got = swap(sent, c=1)
    both = jnp.where(c == 0, jnp.stack([kept, got], axis=1), jnp.stack([got, kept], axis=1))
    return both.reshape(4, PASS // 4, PASS)


def body(gradients, sign_flips):
    outer, dp = lax.axis_index("outer"), lax.axis_index("dp")
    z_high, c = outer // 2, outer % 2
    y, x = dp // 16, dp % 4
    bucket = pltpu.with_memory_space_constraint(gradients.reshape(NY, 4, NX, 2, NC, PASS, PASS), pltpu.HBM)
    h = hadamard(PASS).astype(jnp.bfloat16)
    wide_h = hadamard(2 * PASS).astype(jnp.bfloat16)
    tall_h = jnp.tile(hadamard(HALF) / PASS, (1, 3)).astype(jnp.bfloat16)
    sign = sign_flips.astype(jnp.bfloat16)
    here = jnp.stack([c]).astype(jnp.int32)

    sent = [swap(half, c=1) for half in cut(1 - here, bucket)]
    *own, maximum = rotate_own(here, bucket, sign, wide_h, tall_h)
    mate = []
    for half in sent:
        rotated, maximum = rotate_mate(in_vmem(half), maximum, sign, wide_h, tall_h)
        mate.append(rotated)
    maximum = all_max(maximum)

    table = jnp.stack([orders(g, y, x) for g in range(GROUPS)])
    terms = exchange(reduce_plane(table, maximum, own, mate), "z")
    total, decoded = decode(maximum, sign, h, terms)
    rows = (total / 256.0).reshape(2, 2, PASS // 4, PASS)
    kept, sent = pick(rows, z_high), pick(rows, 1 - z_high)
    line, got = after(exchange(decoded, "z"), swap(sent, z=4))
    mean = mean_rows(kept, got, z_high, c)

    near, far, mean = gather_plane(line, mean)
    own_at = jnp.concatenate([table, jnp.full((1, 8), c, jnp.int32)])
    mate_at = jnp.concatenate([table, jnp.full((1, 8), 1 - c, jnp.int32)])
    near_mates = swap(jnp.stack(near), c=1)
    gradient_sum = assemble(2, own_at, near)
    gradient_sum = assemble(2, mate_at, [near_mates], gradient_sum)
    far_mates = [None] * GROUPS
    for g in (2, 1, 0, 3):
        far[g], gradient_sum = after(far[g], gradient_sum)
        far_mates[g] = swap(far[g], c=1)
    gradient_sum = assemble(0, own_at, far, gradient_sum)
    gradient_sum = assemble(0, mate_at, far_mates, gradient_sum)
    return (mean, gradient_sum.reshape(256, PASS, PASS))


def solution(mesh):
    placed = (P("outer", "dp", None, None, None), P())
    return jax.shard_map(
        body, mesh=mesh, in_specs=placed, out_specs=(P("dp", "outer", None), P()), check_vma=False
    )
```

```python
import functools

import jax
import jax.numpy as jnp
from jax import lax
from jax.experimental import pallas as pl
from jax.experimental.pallas import tpu as pltpu
from jax.sharding import PartitionSpec as P

AXES = ("outer", "dp")
NX, NY, NZ, NC = 4, 4, 8, 2
PASS = 128
VMEM = 16 * 1024 * 1024
HALF = PASS // 2


def coords(index):
    outer, dp = divmod(index, 64)
    return (outer // 2) * 4 + dp // 4 % 4, dp // 16, dp % 4, outer % 2


def linear(z, y, x, c):
    return ((z // 4) * 2 + c) * 64 + (y * 4 + z % 4) * 4 + x


def swap(array, z=0, y=0, x=0, c=0):
    pairs = []
    for index in range(256):
        at = coords(index)
        pairs.append((index, linear(at[0] ^ z, at[1] ^ y, at[2] ^ x, at[3] ^ c)))
    return lax.ppermute(array, AXES, pairs)


def exchange(array, varies):
    groups = {}
    for index in range(256):
        fixed = tuple(at for at, name in zip(coords(index), "zyxc") if name not in varies)
        groups.setdefault(fixed, []).append(index)
    return lax.all_to_all(array, AXES, 0, 0, tiled=True, axis_index_groups=list(groups.values()))


def shift_z(array, step):
    pairs = []
    for index in range(256):
        z, y, x, c = coords(index)
        pairs.append((index, linear((z + step) % NZ, y, x, c)))
    return lax.ppermute(array, AXES, pairs)


def hadamard(length):
    index_row = jnp.arange(length, dtype=jnp.int32)[:, None]
    index_col = jnp.arange(length, dtype=jnp.int32)[None, :]
    common_bits = index_row & index_col
    parity = jnp.zeros((length, length), jnp.int32)
    for bit_pos in range(length.bit_length() - 1):
        parity = parity + (common_bits >> bit_pos & 1)
    return (1 - 2 * (parity % 2)).astype(jnp.float32)


def split3(value):
    high = value.astype(jnp.bfloat16)
    rest = value - high.astype(jnp.float32)
    mid = rest.astype(jnp.bfloat16)
    low = (rest - mid.astype(jnp.float32)).astype(jnp.bfloat16)
    return high, mid, low


def dot(a, b):
    return jnp.dot(a, b, preferred_element_type=jnp.float32)


def params():
    return pltpu.CompilerParams(vmem_limit_bytes=VMEM)


def cost(flops, nbytes):
    return pl.CostEstimate(flops=flops, bytes_accessed=nbytes, transcendentals=0)


def rotate_blocks(blocks, places, sign, wide_h, tall_h, max_ref):
    wide = []
    for block in blocks:
        block = block * sign
        wide.append(jnp.concatenate([block[:HALF], block[HALF:]], axis=1))
    terms = split3(dot(jnp.concatenate(wide, axis=0), wide_h))
    peak = jnp.zeros((8, PASS), jnp.float32)
    for k, (out_ref, at) in enumerate(places):
        rows = slice(k * HALF, (k + 1) * HALF)
        turned = dot(tall_h, jnp.concatenate([term[rows] for term in terms], axis=0))
        for half in range(2):
            part = turned[:, half * PASS : (half + 1) * PASS]
            out_ref[at, half * HALF : (half + 1) * HALF] = part
            peak = jnp.maximum(peak, jnp.max(jnp.abs(part).reshape(8, 8, PASS), axis=0))
    max_ref[...] = jnp.maximum(max_ref[...], peak)


AHEAD = 5


def rotate_own_kernel(core_ref, bucket_ref, sign_ref, wide_ref, tall_ref, low_ref, high_ref, max_ref, held, sems):
    def fetch(step):
        y, x = step // 2, pl.ds(step % 2 * 2, 2)
        return pltpu.make_async_copy(bucket_ref.at[y, :, x, :, core_ref[0]], held.at[step], sems.at[step])

    copies = [fetch(step) for step in range(8)]
    for copy in copies[:AHEAD]:
        copy.start()
    sign, wide_h, tall_h = sign_ref[...], wide_ref[...], tall_ref[...]
    max_ref[...] = jnp.zeros_like(max_ref)
    for step in range(8):
        copies[step].wait()
        if step + AHEAD < 8:
            copies[step + AHEAD].start()
        blocks, places = [], []
        for k in range(16):
            x, high, z = k // 8, k // 4 % 2, k % 4
            blocks.append(held[step, z, x, high])
            places.append(((low_ref, high_ref)[high], (step * 2 + x) * 4 + z))
        rotate_blocks(blocks, places, sign, wide_h, tall_h, max_ref)


def rotate_own(core, bucket, sign, wide_h, tall_h):
    vmem = pl.BlockSpec(memory_space=pltpu.VMEM)
    return pl.pallas_call(
        rotate_own_kernel,
        in_specs=[pl.BlockSpec(memory_space=pltpu.SMEM), pl.BlockSpec(memory_space=pl.ANY), vmem, vmem, vmem],
        out_specs=[vmem] * 3,
        out_shape=[pltpu.VMEM((64, PASS, PASS), jnp.float32)] * 2 + [pltpu.VMEM((8, PASS), jnp.float32)],
        scratch_shapes=[pltpu.VMEM((8, 4, 2, 2, PASS, PASS), jnp.bfloat16), pltpu.SemaphoreType.DMA((8,))],
        compiler_params=params(),
        cost_estimate=cost(8 * 128 * PASS**3, 12 << 20),
        name="rotate_own",
    )(core, bucket, sign, wide_h, tall_h)


def rotate_mate_kernel(half_ref, before_ref, sign_ref, wide_ref, tall_ref, out_ref, max_ref, held, sems):
    copies = [pltpu.make_async_copy(half_ref.at[y], held.at[y], sems.at[y]) for y in range(NY)]
    for copy in copies[:2]:
        copy.start()
    sign, wide_h, tall_h = sign_ref[...], wide_ref[...], tall_ref[...]
    max_ref[...] = before_ref[...]
    for y in range(NY):
        copies[y].wait()
        if y + 2 < NY:
            copies[y + 2].start()
        blocks = [held[y, k % 4, k // 4] for k in range(16)]
        rotate_blocks(blocks, [(out_ref, y * 16 + k) for k in range(16)], sign, wide_h, tall_h, max_ref)


def rotate_mate(half, before, sign, wide_h, tall_h):
    vmem = pl.BlockSpec(memory_space=pltpu.VMEM)
    return pl.pallas_call(
        rotate_mate_kernel,
        in_specs=[pl.BlockSpec(memory_space=pl.ANY)] + [vmem] * 4,
        out_specs=[vmem] * 2,
        out_shape=[pltpu.VMEM((64, PASS, PASS), jnp.float32), pltpu.VMEM((8, PASS), jnp.float32)],
        scratch_shapes=[pltpu.VMEM((NY, 4, NX, PASS, PASS), jnp.bfloat16), pltpu.SemaphoreType.DMA((NY,))],
        compiler_params=params(),
        cost_estimate=cost(4 * 128 * PASS**3, 6 << 20),
        name="rotate_mate",
    )(half, before, sign, wide_h, tall_h)


def cut_kernel(core_ref, bucket_ref, low_ref, high_ref, sems):
    copies = []
    for high, out_ref in enumerate((low_ref, high_ref)):
        for y in range(NY):
            source = bucket_ref.at[y, :, :, high, core_ref[0]]
            copies.append(pltpu.make_async_copy(source, out_ref.at[y], sems.at[len(copies)]))
    for copy in copies:
        copy.start()
    for copy in copies:
        copy.wait()


def cut(core, bucket):
    vmem = pl.BlockSpec(memory_space=pltpu.VMEM)
    return pl.pallas_call(
        cut_kernel,
        in_specs=[pl.BlockSpec(memory_space=pltpu.SMEM), pl.BlockSpec(memory_space=pl.ANY)],
        out_specs=[vmem] * 2,
        out_shape=[jax.ShapeDtypeStruct((NY, 4, NX, PASS, PASS), jnp.bfloat16)] * 2,
        scratch_shapes=[pltpu.SemaphoreType.DMA((2 * NY,))],
        compiler_params=params(),
        cost_estimate=cost(1 << 10, 8 << 20),
        name="cut",
    )(core, bucket)


def max_kernel(whole, *refs):
    value = refs[0][...]
    for ref in refs[1:-1]:
        value = jnp.maximum(value, ref[...])
    refs[-1][...] = jnp.full_like(value, jnp.max(value)) if whole else value


def max_of(*values, whole=False):
    return pl.pallas_call(
        functools.partial(max_kernel, whole),
        out_shape=jax.ShapeDtypeStruct((8, PASS), jnp.float32),
        compiler_params=params(),
        name="max_of",
    )(*values)


def all_max(value):
    value = max_of(value, swap(value, c=1))
    for xor in (1, 3):
        value = max_of(value, swap(value, x=xor), swap(value, y=xor), swap(value, x=xor, y=xor))
    for step in (1, 3):
        value = max_of(value, shift_z(value, step), shift_z(value, -step), whole=step == 3)
    return value


GROUPS = 4


def hops(group):
    return "x" if group < 2 else "y", (1, 3) if group % 2 == 0 else (3, 1)


def orders(group, y, x):
    _, (a, b) = hops(group)
    mine, other = (x, y) if group < 2 else (y, x)
    return jnp.concatenate([mine ^ jnp.array([a, 2, 0, b], jnp.int32), other ^ jnp.array([0, 1, 2, 3], jnp.int32)])


def quantize_kernel(group, start, at_ref, max_ref, own_ref, mate_ref, out_ref):
    scale = 127.0 / max_ref[:1]
    for i in range(2):
        for j in range(4):
            first, second = at_ref[group, start + i], at_ref[group, 4 + j]
            y, x = (second, first) if group < 2 else (first, second)
            for k in range(2):
                b = (y * NX + x) * 4 + 2 * group % 4 + k
                code = jnp.floor(own_ref[b] * scale + 0.5) + jnp.floor(mate_ref[b] * scale + 0.5)
                out_ref[i, j, k] = code.astype(jnp.bfloat16)


def in_vmem(array):
    return pltpu.with_memory_space_constraint(array, pltpu.VMEM)


def quantize(group, start, table, maximum, own, mate):
    vmem = pl.BlockSpec(memory_space=pltpu.VMEM)
    return pl.pallas_call(
        functools.partial(quantize_kernel, group, start),
        in_specs=[pl.BlockSpec(memory_space=pltpu.SMEM), vmem, vmem, vmem],
        out_specs=vmem,
        out_shape=jax.ShapeDtypeStruct((2, 4, 2, PASS, PASS), jnp.bfloat16),
        compiler_params=params(),
        cost_estimate=cost(1 << 21, 5 << 19),
        name="quantize",
    )(table, maximum, own, mate)


def add_first_kernel(kept_ref, got_ref, low_ref, high_ref):
    for start, out_ref in ((0, low_ref), (1, high_ref)):
        total = kept_ref[start].astype(jnp.int32) + got_ref[start].astype(jnp.int32)
        out_ref[...] = total.astype(jnp.int16)


def add_first(kept, got):
    return pl.pallas_call(
        add_first_kernel,
        out_shape=[jax.ShapeDtypeStruct(kept.shape[1:], jnp.int16)] * 2,
        compiler_params=params(),
        cost_estimate=cost(kept.size, kept.size * 6),
        name="add_first",
    )(kept, got)


def add_pair_kernel(*refs):
    for g in range(2):
        total = refs[2 * g][...].astype(jnp.int32) + refs[2 * g + 1][...].astype(jnp.int32)
        total = total.astype(jnp.int16)
        for k in range(4):
            refs[4 + k][2 * g : 2 * g + 2] = total[k]


def add_pair(terms):
    return pl.pallas_call(
        add_pair_kernel,
        out_shape=[jax.ShapeDtypeStruct((4, PASS, PASS), jnp.int16)] * 4,
        compiler_params=params(),
        cost_estimate=cost(1 << 19, 3 << 19),
        name="add_pair",
    )(*terms)


def add_last_kernel(*refs):
    for pair in range(2):
        total = refs[4 * pair][...].astype(jnp.int32)
        for k in range(1, 4):
            total = total + refs[4 * pair + k][...].astype(jnp.int32)
        refs[-1][4 * pair : 4 * pair + 4] = total.astype(jnp.int16)


def add_last(terms):
    return pl.pallas_call(
        add_last_kernel,
        out_shape=jax.ShapeDtypeStruct((NZ, PASS, PASS), jnp.int16),
        compiler_params=params(),
        cost_estimate=cost(1 << 18, 3 << 18),
        name="add_last",
    )(*terms)


def spread(array, axis):
    return [swap(array[k] if isinstance(array, (list, tuple)) else array, **{axis: k}) for k in range(1, 4)]


def reduce_plane(table, maximum, own, mate):
    parts = [
        [quantize(g, start, table, maximum, in_vmem(own[g // 2]), in_vmem(mate[g // 2])) for start in (0, 2)]
        for g in range(GROUPS)
    ]
    for hop in range(2):
        got = []
        for g in range(GROUPS):
            axis, xors = hops(g)
            got.append(swap(parts[g][0], **{axis: xors[hop]}))
        if hop == 0:
            parts = [add_first(parts[g][1], got[g])[::-1] for g in range(GROUPS)]
    terms = []
    for pair, axis in enumerate(("y", "x")):
        cuts = add_pair([t for g in (2 * pair, 2 * pair + 1) for t in (parts[g][1], got[g])])
        terms += [cuts[0], *spread(cuts, axis)]
    return add_last(terms)


def gather_plane(line):
    terms = []
    for pair, axis in enumerate(("y", "x")):
        part = line[4 * pair : 4 * pair + 4]
        terms += [part, *spread(part, axis)]
    held = deal(terms)
    for hop in (1, 0):
        got = []
        for g in range(GROUPS):
            axis, xors = hops(g)
            got.append(swap(held[g], **{axis: xors[hop]}))
        if hop == 1:
            held = [jnp.concatenate([held[g], got[g]], axis=0) for g in range(GROUPS)]
    return held, got


def placements(at_ref, start, piece, out_ref, sems):
    copies = []
    for g in range(GROUPS):
        for i in range(2):
            for j in range(4):
                first, second = at_ref[g, start + i], at_ref[g, 4 + j]
                y, x = (second, first) if g < 2 else (first, second)
                place = out_ref.at[y, pl.ds(2 * g % 4, 2), x, g // 2, at_ref[GROUPS, 0]]
                copies.append(pltpu.make_async_copy(piece(g, i, j), place, sems.at[len(copies)]))
    return copies


def assemble_kernel(start, count, at_ref, *refs):
    pieces, out_ref, sems = refs[:count], refs[-2], refs[-1]

    def piece(g, i, j):
        return pieces[g].at[i, j] if count > 1 else pieces[0].at[g, i, j]

    copies = placements(at_ref, start, piece, out_ref, sems)
    for copy in copies:
        copy.start()
    for copy in copies:
        copy.wait()


def assemble(start, at, pieces, before=None):
    more = [] if before is None else [before]
    anywhere = pl.BlockSpec(memory_space=pl.ANY)
    return pl.pallas_call(
        functools.partial(assemble_kernel, start, len(pieces)),
        in_specs=[pl.BlockSpec(memory_space=pltpu.SMEM)]
        + [pl.BlockSpec(memory_space=pltpu.VMEM)] * len(pieces)
        + [anywhere] * len(more),
        out_specs=anywhere,
        out_shape=jax.ShapeDtypeStruct((NY, 4, NX, 2, NC, PASS, PASS), jnp.bfloat16),
        scratch_shapes=[pltpu.SemaphoreType.DMA((8 * GROUPS,))],
        input_output_aliases={1 + len(pieces): 0} if more else {},
        compiler_params=params(),
        cost_estimate=cost(1 << 10, 4 << 20),
        name="assemble",
    )(at, *pieces, *more)


def decode_kernel(max_ref, sign_ref, h_ref, terms_ref, total_ref, out_ref):
    total = terms_ref[0].astype(jnp.int32)
    for k in range(1, NZ):
        total = total + terms_ref[k].astype(jnp.int32)
    total = total.astype(jnp.float32)
    total_ref[...] = total
    h = h_ref[...]
    high, mid, low = split3(total)
    first = dot(high, h) + (dot(mid, h) + dot(low, h))
    high, mid, low = split3(first)
    second = dot(h, high) + (dot(h, mid) + dot(h, low))
    unit = max_ref[:1] / (127.0 * PASS)
    decoded = (second * sign_ref[...].astype(jnp.float32) * unit).astype(jnp.bfloat16)
    for k in range(NZ):
        out_ref[k] = decoded


def decode(maximum, sign, h, terms):
    return pl.pallas_call(
        decode_kernel,
        out_shape=[
            jax.ShapeDtypeStruct((PASS, PASS), jnp.float32),
            jax.ShapeDtypeStruct((NZ, PASS, PASS), jnp.bfloat16),
        ],
        compiler_params=params(),
        cost_estimate=cost(12 * PASS**3, 1 << 19),
        name="decode",
    )(maximum, sign, h, terms)


def deal_kernel(*refs):
    for g in range(GROUPS):
        for k in range(4):
            refs[8 + g][0, k] = refs[g // 2 * 4 + k][2 * (g % 2) : 2 * (g % 2) + 2]


def deal(terms):
    return pl.pallas_call(
        deal_kernel,
        out_shape=[jax.ShapeDtypeStruct((1, 4, 2, PASS, PASS), jnp.bfloat16)] * GROUPS,
        compiler_params=params(),
        cost_estimate=cost(1 << 10, 1 << 21),
        name="deal",
    )(*terms)


def after_kernel(*refs):
    pass


def after(array, before):
    anywhere = pl.BlockSpec(memory_space=pl.ANY)
    return pl.pallas_call(
        after_kernel,
        in_specs=[anywhere] * 2,
        out_specs=[anywhere] * 2,
        out_shape=[jax.ShapeDtypeStruct(a.shape, a.dtype) for a in (array, before)],
        input_output_aliases={0: 0, 1: 1},
        compiler_params=params(),
        name="after",
    )(array, before)


def pick(pair, index):
    return jnp.where(index == 0, pair[0], pair[1])


def place(kept, got, index, axis):
    return jnp.where(index == 0, jnp.stack([kept, got], axis), jnp.stack([got, kept], axis))


def body(gradients, sign_flips):
    outer, dp = lax.axis_index("outer"), lax.axis_index("dp")
    z_high, c = outer // 2, outer % 2
    y, x = dp // 16, dp % 4
    bucket = pltpu.with_memory_space_constraint(gradients.reshape(NY, 4, NX, 2, NC, PASS, PASS), pltpu.HBM)
    h = hadamard(PASS).astype(jnp.bfloat16)
    wide_h = hadamard(2 * PASS).astype(jnp.bfloat16)
    tall_h = jnp.tile(hadamard(HALF) / PASS, (1, 3)).astype(jnp.bfloat16)
    sign = sign_flips.astype(jnp.bfloat16)
    here = jnp.stack([c]).astype(jnp.int32)

    sent = [swap(half, c=1) for half in cut(1 - here, bucket)]
    *own, maximum = rotate_own(here, bucket, sign, wide_h, tall_h)
    mate = []
    for half in sent:
        rotated, maximum = rotate_mate(half, maximum, sign, wide_h, tall_h)
        mate.append(rotated)
    maximum = all_max(maximum)

    table = jnp.stack([orders(g, y, x) for g in range(GROUPS)])
    terms = exchange(reduce_plane(table, maximum, own, mate), "z")
    total, decoded = decode(maximum, sign, h, terms)
    rows = (total / 256.0).reshape(2, 2, PASS // 4, PASS).swapaxes(0, 1)
    near, far = gather_plane(exchange(decoded, "z"))
    own_at = jnp.concatenate([table, jnp.full((1, 8), c, jnp.int32)])
    mate_at = jnp.concatenate([table, jnp.full((1, 8), 1 - c, jnp.int32)])
    near_mates = swap(jnp.stack(near), c=1)
    gradient_sum = assemble(2, own_at, near)
    gradient_sum = assemble(2, mate_at, [near_mates], gradient_sum)
    sent, gradient_sum = after(pick(rows, 1 - c), gradient_sum)
    rows = place(pick(rows, c), swap(sent, c=1), c, 1)
    mean = place(pick(rows, z_high), swap(pick(rows, 1 - z_high), z=4), z_high, 0)
    far[3], mean = after(far[3], mean)
    far_mates = [None] * GROUPS
    for g in (2, 1, 0, 3):
        far[g], gradient_sum = after(far[g], gradient_sum)
        far_mates[g] = swap(far[g], c=1)
    gradient_sum = assemble(0, own_at, far, gradient_sum)
    gradient_sum = assemble(0, mate_at, far_mates, gradient_sum)
    return (mean.reshape(4, PASS // 4, PASS), gradient_sum.reshape(256, PASS, PASS))


def solution(mesh):
    placed = (P("outer", "dp", None, None, None), P())
    return jax.shard_map(
        body, mesh=mesh, in_specs=placed, out_specs=(P("dp", "outer", None), P()), check_vma=False
    )
```

```python
import functools

import jax
import jax.numpy as jnp
from jax import lax
from jax.experimental import pallas as pl
from jax.experimental.pallas import tpu as pltpu
from jax.sharding import PartitionSpec as P

AXES = ("outer", "dp")
NX, NY, NZ, NC = 4, 4, 8, 2
PASS = 128
VMEM = 16 * 1024 * 1024
HALF = PASS // 2


def coords(index):
    outer, dp = divmod(index, 64)
    return (outer // 2) * 4 + dp // 4 % 4, dp // 16, dp % 4, outer % 2


def linear(z, y, x, c):
    return ((z // 4) * 2 + c) * 64 + (y * 4 + z % 4) * 4 + x


def swap(array, z=0, y=0, x=0, c=0):
    pairs = []
    for index in range(256):
        at = coords(index)
        pairs.append((index, linear(at[0] ^ z, at[1] ^ y, at[2] ^ x, at[3] ^ c)))
    return lax.ppermute(array, AXES, pairs)


def exchange(array, varies):
    groups = {}
    for index in range(256):
        fixed = tuple(at for at, name in zip(coords(index), "zyxc") if name not in varies)
        groups.setdefault(fixed, []).append(index)
    return lax.all_to_all(array, AXES, 0, 0, tiled=True, axis_index_groups=list(groups.values()))


def shift_z(array, step):
    pairs = []
    for index in range(256):
        z, y, x, c = coords(index)
        pairs.append((index, linear((z + step) % NZ, y, x, c)))
    return lax.ppermute(array, AXES, pairs)


def hadamard(length):
    index_row = jnp.arange(length, dtype=jnp.int32)[:, None]
    index_col = jnp.arange(length, dtype=jnp.int32)[None, :]
    common_bits = index_row & index_col
    parity = jnp.zeros((length, length), jnp.int32)
    for bit_pos in range(length.bit_length() - 1):
        parity = parity + (common_bits >> bit_pos & 1)
    return (1 - 2 * (parity % 2)).astype(jnp.float32)


def split3(value):
    high = value.astype(jnp.bfloat16)
    rest = value - high.astype(jnp.float32)
    mid = rest.astype(jnp.bfloat16)
    low = (rest - mid.astype(jnp.float32)).astype(jnp.bfloat16)
    return high, mid, low


def dot(a, b):
    return jnp.dot(a, b, preferred_element_type=jnp.float32)


def params():
    return pltpu.CompilerParams(vmem_limit_bytes=VMEM)


def cost(flops, nbytes):
    return pl.CostEstimate(flops=flops, bytes_accessed=nbytes, transcendentals=0)


def rotate_blocks(blocks, places, sign, wide_h, tall_h, max_ref):
    wide = []
    for block in blocks:
        block = block * sign
        wide.append(jnp.concatenate([block[:HALF], block[HALF:]], axis=1))
    terms = split3(dot(jnp.concatenate(wide, axis=0), wide_h))
    peak = jnp.zeros((8, PASS), jnp.float32)
    for k, (out_ref, at) in enumerate(places):
        rows = slice(k * HALF, (k + 1) * HALF)
        turned = dot(tall_h, jnp.concatenate([term[rows] for term in terms], axis=0))
        for half in range(2):
            part = turned[:, half * PASS : (half + 1) * PASS]
            out_ref[at, half * HALF : (half + 1) * HALF] = part
            peak = jnp.maximum(peak, jnp.max(jnp.abs(part).reshape(8, 8, PASS), axis=0))
    max_ref[...] = jnp.maximum(max_ref[...], peak)


AHEAD = 5


def rotate_own_kernel(core_ref, bucket_ref, sign_ref, wide_ref, tall_ref, low_ref, high_ref, max_ref, held, sems):
    def fetch(step):
        y, x = step // 2, pl.ds(step % 2 * 2, 2)
        return pltpu.make_async_copy(bucket_ref.at[y, :, x, :, core_ref[0]], held.at[step], sems.at[step])

    copies = [fetch(step) for step in range(8)]
    for copy in copies[:AHEAD]:
        copy.start()
    sign, wide_h, tall_h = sign_ref[...], wide_ref[...], tall_ref[...]
    max_ref[...] = jnp.zeros_like(max_ref)
    for step in range(8):
        copies[step].wait()
        if step + AHEAD < 8:
            copies[step + AHEAD].start()
        blocks, places = [], []
        for k in range(16):
            x, high, z = k // 8, k // 4 % 2, k % 4
            blocks.append(held[step, z, x, high])
            places.append(((low_ref, high_ref)[high], (step * 2 + x) * 4 + z))
        rotate_blocks(blocks, places, sign, wide_h, tall_h, max_ref)


def rotate_own(core, bucket, sign, wide_h, tall_h):
    vmem = pl.BlockSpec(memory_space=pltpu.VMEM)
    return pl.pallas_call(
        rotate_own_kernel,
        in_specs=[pl.BlockSpec(memory_space=pltpu.SMEM), pl.BlockSpec(memory_space=pl.ANY), vmem, vmem, vmem],
        out_specs=[vmem] * 3,
        out_shape=[pltpu.VMEM((64, PASS, PASS), jnp.float32)] * 2 + [pltpu.VMEM((8, PASS), jnp.float32)],
        scratch_shapes=[pltpu.VMEM((8, 4, 2, 2, PASS, PASS), jnp.bfloat16), pltpu.SemaphoreType.DMA((8,))],
        compiler_params=params(),
        cost_estimate=cost(8 * 128 * PASS**3, 12 << 20),
        name="rotate_own",
    )(core, bucket, sign, wide_h, tall_h)


def rotate_mate_kernel(half_ref, before_ref, sign_ref, wide_ref, tall_ref, out_ref, max_ref, held, sems):
    copies = [pltpu.make_async_copy(half_ref.at[y], held.at[y], sems.at[y]) for y in range(NY)]
    for copy in copies[:2]:
        copy.start()
    sign, wide_h, tall_h = sign_ref[...], wide_ref[...], tall_ref[...]
    max_ref[...] = before_ref[...]
    for y in range(NY):
        copies[y].wait()
        if y + 2 < NY:
            copies[y + 2].start()
        blocks = [held[y, k % 4, k // 4] for k in range(16)]
        rotate_blocks(blocks, [(out_ref, y * 16 + k) for k in range(16)], sign, wide_h, tall_h, max_ref)


def rotate_mate(half, before, sign, wide_h, tall_h):
    vmem = pl.BlockSpec(memory_space=pltpu.VMEM)
    return pl.pallas_call(
        rotate_mate_kernel,
        in_specs=[pl.BlockSpec(memory_space=pl.ANY)] + [vmem] * 4,
        out_specs=[vmem] * 2,
        out_shape=[pltpu.VMEM((64, PASS, PASS), jnp.float32), pltpu.VMEM((8, PASS), jnp.float32)],
        scratch_shapes=[pltpu.VMEM((NY, 4, NX, PASS, PASS), jnp.bfloat16), pltpu.SemaphoreType.DMA((NY,))],
        compiler_params=params(),
        cost_estimate=cost(4 * 128 * PASS**3, 6 << 20),
        name="rotate_mate",
    )(half, before, sign, wide_h, tall_h)


def cut_kernel(core_ref, bucket_ref, low_ref, high_ref, sems):
    copies = []
    for high, out_ref in enumerate((low_ref, high_ref)):
        for y in range(NY):
            source = bucket_ref.at[y, :, :, high, core_ref[0]]
            copies.append(pltpu.make_async_copy(source, out_ref.at[y], sems.at[len(copies)]))
    for copy in copies:
        copy.start()
    for copy in copies:
        copy.wait()


def cut(core, bucket):
    vmem = pl.BlockSpec(memory_space=pltpu.VMEM)
    return pl.pallas_call(
        cut_kernel,
        in_specs=[pl.BlockSpec(memory_space=pltpu.SMEM), pl.BlockSpec(memory_space=pl.ANY)],
        out_specs=[vmem] * 2,
        out_shape=[jax.ShapeDtypeStruct((NY, 4, NX, PASS, PASS), jnp.bfloat16)] * 2,
        scratch_shapes=[pltpu.SemaphoreType.DMA((2 * NY,))],
        compiler_params=params(),
        cost_estimate=cost(1 << 10, 8 << 20),
        name="cut",
    )(core, bucket)


def max_kernel(whole, *refs):
    value = refs[0][...]
    for ref in refs[1:-1]:
        value = jnp.maximum(value, ref[...])
    refs[-1][...] = jnp.full_like(value, jnp.max(value)) if whole else value


def max_of(*values, whole=False):
    return pl.pallas_call(
        functools.partial(max_kernel, whole),
        out_shape=jax.ShapeDtypeStruct((8, PASS), jnp.float32),
        compiler_params=params(),
        name="max_of",
    )(*values)


def all_max(value):
    value = max_of(value, swap(value, c=1))
    for xor in (1, 3):
        value = max_of(value, swap(value, x=xor), swap(value, y=xor), swap(value, x=xor, y=xor))
    for step in (1, 3):
        value = max_of(value, shift_z(value, step), shift_z(value, -step), whole=step == 3)
    return value


GROUPS = 4


def hops(group):
    return "x" if group < 2 else "y", (1, 3) if group % 2 == 0 else (3, 1)


def orders(group, y, x):
    _, (a, b) = hops(group)
    mine, other = (x, y) if group < 2 else (y, x)
    return jnp.concatenate([mine ^ jnp.array([a, 2, 0, b], jnp.int32), other ^ jnp.array([0, 1, 2, 3], jnp.int32)])


def quantize_kernel(group, start, at_ref, max_ref, own_ref, mate_ref, out_ref):
    scale = 127.0 / max_ref[:1]
    for i in range(2):
        for j in range(4):
            first, second = at_ref[group, start + i], at_ref[group, 4 + j]
            y, x = (second, first) if group < 2 else (first, second)
            for k in range(2):
                b = (y * NX + x) * 4 + 2 * group % 4 + k
                code = jnp.floor(own_ref[b] * scale + 0.5) + jnp.floor(mate_ref[b] * scale + 0.5)
                out_ref[i, j, k] = code.astype(jnp.bfloat16)


def in_vmem(array):
    return pltpu.with_memory_space_constraint(array, pltpu.VMEM)


def quantize(group, start, table, maximum, own, mate):
    vmem = pl.BlockSpec(memory_space=pltpu.VMEM)
    return pl.pallas_call(
        functools.partial(quantize_kernel, group, start),
        in_specs=[pl.BlockSpec(memory_space=pltpu.SMEM), vmem, vmem, vmem],
        out_specs=vmem,
        out_shape=jax.ShapeDtypeStruct((2, 4, 2, PASS, PASS), jnp.bfloat16),
        compiler_params=params(),
        cost_estimate=cost(1 << 21, 5 << 19),
        name="quantize",
    )(table, maximum, own, mate)


def add_first_kernel(kept_ref, got_ref, low_ref, high_ref):
    for start, out_ref in ((0, low_ref), (1, high_ref)):
        total = kept_ref[start].astype(jnp.int32) + got_ref[start].astype(jnp.int32)
        out_ref[...] = total.astype(jnp.int16)


def add_first(kept, got):
    return pl.pallas_call(
        add_first_kernel,
        out_shape=[jax.ShapeDtypeStruct(kept.shape[1:], jnp.int16)] * 2,
        compiler_params=params(),
        cost_estimate=cost(kept.size, kept.size * 6),
        name="add_first",
    )(kept, got)


def add_pair_kernel(*refs):
    for g in range(2):
        total = refs[2 * g][...].astype(jnp.int32) + refs[2 * g + 1][...].astype(jnp.int32)
        total = total.astype(jnp.int16)
        for k in range(4):
            refs[4 + k][2 * g : 2 * g + 2] = total[k]


def add_pair(terms):
    return pl.pallas_call(
        add_pair_kernel,
        out_shape=[jax.ShapeDtypeStruct((4, PASS, PASS), jnp.int16)] * 4,
        compiler_params=params(),
        cost_estimate=cost(1 << 19, 3 << 19),
        name="add_pair",
    )(*terms)


def add_last_kernel(*refs):
    for pair in range(2):
        total = refs[4 * pair][...].astype(jnp.int32)
        for k in range(1, 4):
            total = total + refs[4 * pair + k][...].astype(jnp.int32)
        refs[-1][4 * pair : 4 * pair + 4] = total.astype(jnp.int16)


def add_last(terms):
    return pl.pallas_call(
        add_last_kernel,
        out_shape=jax.ShapeDtypeStruct((NZ, PASS, PASS), jnp.int16),
        compiler_params=params(),
        cost_estimate=cost(1 << 18, 3 << 18),
        name="add_last",
    )(*terms)


def spread(array, axis):
    return [swap(array[k] if isinstance(array, (list, tuple)) else array, **{axis: k}) for k in range(1, 4)]


def reduce_plane(table, maximum, own, mate):
    parts = [
        [quantize(g, start, table, maximum, in_vmem(own[g // 2]), in_vmem(mate[g // 2])) for start in (0, 2)]
        for g in range(GROUPS)
    ]
    for hop in range(2):
        got = []
        for g in range(GROUPS):
            axis, xors = hops(g)
            got.append(swap(parts[g][0], **{axis: xors[hop]}))
        if hop == 0:
            parts = [add_first(parts[g][1], got[g])[::-1] for g in range(GROUPS)]
    terms = []
    for pair, axis in enumerate(("y", "x")):
        cuts = add_pair([t for g in (2 * pair, 2 * pair + 1) for t in (parts[g][1], got[g])])
        terms += [cuts[0], *spread(cuts, axis)]
    return add_last(terms)


def gather_plane(line):
    terms = []
    for pair, axis in enumerate(("y", "x")):
        part = line[4 * pair : 4 * pair + 4]
        terms += [part, *spread(part, axis)]
    held = deal(terms)
    for hop in (1, 0):
        got = []
        for g in range(GROUPS):
            axis, xors = hops(g)
            got.append(swap(held[g], **{axis: xors[hop]}))
        if hop == 1:
            held = [jnp.concatenate([held[g], got[g]], axis=0) for g in range(GROUPS)]
    return held, got


def placements(at_ref, start, piece, out_ref, sems):
    copies = []
    for g in range(GROUPS):
        for i in range(2):
            for j in range(4):
                first, second = at_ref[g, start + i], at_ref[g, 4 + j]
                y, x = (second, first) if g < 2 else (first, second)
                place = out_ref.at[y, pl.ds(2 * g % 4, 2), x, g // 2, at_ref[GROUPS, 0]]
                copies.append(pltpu.make_async_copy(piece(g, i, j), place, sems.at[len(copies)]))
    return copies


def assemble_kernel(start, count, at_ref, *refs):
    pieces, out_ref, sems = refs[:count], refs[-2], refs[-1]

    def piece(g, i, j):
        return pieces[g].at[i, j] if count > 1 else pieces[0].at[g, i, j]

    copies = placements(at_ref, start, piece, out_ref, sems)
    for copy in copies:
        copy.start()
    for copy in copies:
        copy.wait()


def assemble(start, at, pieces, before=None):
    more = [] if before is None else [before]
    anywhere = pl.BlockSpec(memory_space=pl.ANY)
    return pl.pallas_call(
        functools.partial(assemble_kernel, start, len(pieces)),
        in_specs=[pl.BlockSpec(memory_space=pltpu.SMEM)]
        + [pl.BlockSpec(memory_space=pltpu.VMEM)] * len(pieces)
        + [anywhere] * len(more),
        out_specs=anywhere,
        out_shape=jax.ShapeDtypeStruct((NY, 4, NX, 2, NC, PASS, PASS), jnp.bfloat16),
        scratch_shapes=[pltpu.SemaphoreType.DMA((8 * GROUPS,))],
        input_output_aliases={1 + len(pieces): 0} if more else {},
        compiler_params=params(),
        cost_estimate=cost(1 << 10, 4 << 20),
        name="assemble",
    )(at, *pieces, *more)


def decode_kernel(max_ref, sign_ref, h_ref, terms_ref, total_ref, out_ref):
    total = terms_ref[0].astype(jnp.int32)
    for k in range(1, NZ):
        total = total + terms_ref[k].astype(jnp.int32)
    total = total.astype(jnp.float32)
    total_ref[...] = total
    h = h_ref[...]
    high, mid, low = split3(total)
    first = dot(high, h) + (dot(mid, h) + dot(low, h))
    high, mid, low = split3(first)
    second = dot(h, high) + (dot(h, mid) + dot(h, low))
    unit = max_ref[:1] / (127.0 * PASS)
    decoded = (second * sign_ref[...].astype(jnp.float32) * unit).astype(jnp.bfloat16)
    for k in range(NZ):
        out_ref[k] = decoded


def decode(maximum, sign, h, terms):
    return pl.pallas_call(
        decode_kernel,
        out_shape=[
            jax.ShapeDtypeStruct((PASS, PASS), jnp.float32),
            jax.ShapeDtypeStruct((NZ, PASS, PASS), jnp.bfloat16),
        ],
        compiler_params=params(),
        cost_estimate=cost(12 * PASS**3, 1 << 19),
        name="decode",
    )(maximum, sign, h, terms)


def deal_kernel(*refs):
    for g in range(GROUPS):
        for k in range(4):
            refs[8 + g][0, k] = refs[g // 2 * 4 + k][2 * (g % 2) : 2 * (g % 2) + 2]


def deal(terms):
    return pl.pallas_call(
        deal_kernel,
        out_shape=[jax.ShapeDtypeStruct((1, 4, 2, PASS, PASS), jnp.bfloat16)] * GROUPS,
        compiler_params=params(),
        cost_estimate=cost(1 << 10, 1 << 21),
        name="deal",
    )(*terms)


def after_kernel(*refs):
    pass


def after(array, before):
    anywhere = pl.BlockSpec(memory_space=pl.ANY)
    return pl.pallas_call(
        after_kernel,
        in_specs=[anywhere] * 2,
        out_specs=[anywhere] * 2,
        out_shape=[jax.ShapeDtypeStruct(a.shape, a.dtype) for a in (array, before)],
        input_output_aliases={0: 0, 1: 1},
        compiler_params=params(),
        name="after",
    )(array, before)


def pick(pair, index):
    return jnp.where(index == 0, pair[0], pair[1])


def once(array, before):
    anywhere = pl.BlockSpec(memory_space=pl.ANY)
    return pl.pallas_call(
        after_kernel,
        in_specs=[anywhere] * 2,
        out_specs=anywhere,
        out_shape=jax.ShapeDtypeStruct(array.shape, array.dtype),
        input_output_aliases={0: 0},
        compiler_params=params(),
        name="once",
    )(array, before)


def place(kept, got, index, axis):
    return jnp.where(index == 0, jnp.stack([kept, got], axis), jnp.stack([got, kept], axis))


def body(gradients, sign_flips):
    outer, dp = lax.axis_index("outer"), lax.axis_index("dp")
    z_high, c = outer // 2, outer % 2
    y, x = dp // 16, dp % 4
    bucket = pltpu.with_memory_space_constraint(gradients.reshape(NY, 4, NX, 2, NC, PASS, PASS), pltpu.HBM)
    h = hadamard(PASS).astype(jnp.bfloat16)
    wide_h = hadamard(2 * PASS).astype(jnp.bfloat16)
    tall_h = jnp.tile(hadamard(HALF) / PASS, (1, 3)).astype(jnp.bfloat16)
    sign = sign_flips.astype(jnp.bfloat16)
    here = jnp.stack([c]).astype(jnp.int32)

    sent = [swap(half, c=1) for half in cut(1 - here, bucket)]
    *own, maximum = rotate_own(here, bucket, sign, wide_h, tall_h)
    mate = []
    for half in sent:
        rotated, maximum = rotate_mate(half, maximum, sign, wide_h, tall_h)
        mate.append(rotated)
    maximum = all_max(maximum)

    table = jnp.stack([orders(g, y, x) for g in range(GROUPS)])
    terms = exchange(reduce_plane(table, maximum, own, mate), "z")
    total, decoded = decode(maximum, sign, h, terms)
    rows = (total / 256.0).reshape(2, 2, PASS // 4, PASS).swapaxes(0, 1)
    near, far = gather_plane(exchange(decoded, "z"))
    own_at = jnp.concatenate([table, jnp.full((1, 8), c, jnp.int32)])
    mate_at = jnp.concatenate([table, jnp.full((1, 8), 1 - c, jnp.int32)])
    near_mates = swap(jnp.stack(near), c=1)
    sent = once(pick(rows, 1 - c), near_mates)
    gradient_sum = assemble(2, own_at, near)
    gradient_sum = assemble(2, mate_at, [near_mates], gradient_sum)
    rows = place(pick(rows, c), swap(sent, c=1), c, 1)
    mean = place(pick(rows, z_high), swap(pick(rows, 1 - z_high), z=4), z_high, 0)
    far[3], mean = after(far[3], mean)
    far_mates = [None] * GROUPS
    for g in (2, 1, 0, 3):
        far[g], gradient_sum = after(far[g], gradient_sum)
        far_mates[g] = swap(far[g], c=1)
    gradient_sum = assemble(0, own_at, far, gradient_sum)
    gradient_sum = assemble(0, mate_at, far_mates, gradient_sum)
    return (mean.reshape(4, PASS // 4, PASS), gradient_sum.reshape(256, PASS, PASS))


def solution(mesh):
    placed = (P("outer", "dp", None, None, None), P())
    return jax.shard_map(
        body, mesh=mesh, in_specs=placed, out_specs=(P("dp", "outer", None), P()), check_vma=False
    )
```
